32 devices in a mesh: dp: 2 (over core), seq: 16 (over z, y, x).
Axes of the slice: x: 2, y: 2, z: 4, core: 2. Of those that a mesh axis runs over, the one named last changes fastest.
Arguments:
- queries: bfloat16 [2, 2048, 2048], P('dp', 'seq'), may hold values from -62 to 62
- keys: bfloat16 [2, 2048, 2048], P('dp', 'seq'), may hold values from -4 to 4
- values: bfloat16 [2, 2048, 2048], P('dp', 'seq'), may hold values from -4 to 4
- cotangent: bfloat16 [2, 2048, 2048], P('dp', 'seq'), may hold values from -4 to 4
- cluster_of: int32 [2, 16, 32], P('dp', None, 'seq'), may hold values from 0 to 127, as said below
- block_list: int32 [2, 2048, 4], P('dp', 'seq'), may hold values from -1 to 31, as said below
- centroid_sums: float32 [2048, 128], P('seq'), may hold values from -5 to 5
Outputs:
- attn_out: bfloat16 [2, 2048, 2048], P('dp', 'seq')
- grad_q: bfloat16 [2, 2048, 2048], P('dp', 'seq')
- grad_k: bfloat16 [2, 2048, 2048], P('dp', 'seq')
- grad_v: bfloat16 [2, 2048, 2048], P('dp', 'seq')
- centroid_next: float32 [2048, 128], P('seq')
The draws below stay inside these ranges and needn't reach their ends.
Inputs may be any that keep to these rules, and one draw needn't show every extreme that they name: cluster_of[d, h, b] is the cluster under head h of block b of document d; the centroid of cluster c of head h lies on seq index h + c // 128. Of the 2 blocks on one seq index, at most 2 share the value c // 128 under one head, and in every draw some reach 2. Row h * 128 + c of block_list[d] lists in increasing order the blocks b with cluster_of[d, h, b] == c, then -1; every block appears once for each head; a cluster holds at most 4 blocks, and in every draw some cluster holds exactly 4.
All inputs are finite; a program needn't handle non-finite values.
Results may differ from the reference program's by a relative error of at most 0.015.
Values may be sent and summed in bfloat16 or wider, within the bound.
A program may use at most 128 MiB of HBM per device.

```python
import math
import jax
import jax.numpy as jnp
from jax import lax

HEADS = 16
HD = 128
CENT = 128
BLK = 64
DOCS = 2
TOKENS = 2048
BLOCKS = 32
BLK_DEV = 2
OWN_H = 1
CL_DEV = 128
CAP = 2
MOST = 4
N_SEQ = 16


def route_tables(base_key):
    key_owner = jax.random.fold_in(base_key, 701)
    key_forced = jax.random.fold_in(base_key, 702)
    key_first = jax.random.fold_in(base_key, 703)
    key_order = jax.random.fold_in(base_key, 704)
    key_full = jax.random.fold_in(base_key, 705)
    key_slots = jax.random.fold_in(base_key, 706)
    owner_keys = jax.random.split(key_owner, DOCS * HEADS * N_SEQ)
    drawn = jax.vmap(lambda single: jax.random.permutation(single, OWN_H * CAP)[:BLK_DEV])(owner_keys)
    owner_local = (drawn // CAP).astype(jnp.int32).reshape(DOCS, HEADS, N_SEQ, BLK_DEV)
    forced_owner = jax.random.randint(key_forced, (DOCS, HEADS, 1, 1), 0, OWN_H)
    first_device = jax.random.randint(key_first, (DOCS, HEADS, 1), 0, N_SEQ)
    device_ids = jnp.arange(N_SEQ, dtype=jnp.int32)[None, None, :]
    forced_device = (device_ids - first_device) % N_SEQ < MOST
    rotated = (jnp.arange(BLK_DEV, dtype=jnp.int32)[None, None, None, :] // CAP + forced_owner) % OWN_H
    owner_local = jnp.where(forced_device[..., None], rotated, owner_local).reshape(DOCS, HEADS, BLOCKS)
    block_first = (jnp.arange(BLK_DEV, dtype=jnp.int32) == 0)[None, None, None, :]
    forced_block = (forced_device[..., None] & block_first).reshape(DOCS, HEADS, BLOCKS)
    order_key = jax.random.randint(key_order, (DOCS, HEADS, BLOCKS), 0, 1 << 20)
    order_key = jnp.where(forced_block, 0, order_key + 1)
    block_ids = jnp.arange(BLOCKS, dtype=jnp.int32)

    def rank_one(packed):
        owners, order_row = packed
        same_owner = owners[None, :] == owners[:, None]
        earlier = (order_row[None, :] < order_row[:, None]) | (order_row[None, :] == order_row[:, None]) & (block_ids[None, :] < block_ids[:, None])
        return jnp.sum(same_owner & earlier, axis=1).astype(jnp.int32)
    rank_at = lax.map(rank_one, (owner_local.reshape(-1, BLOCKS), order_key.reshape(-1, BLOCKS))).reshape(DOCS, HEADS, BLOCKS)
    full_cluster = jax.random.randint(key_full, (DOCS, HEADS, OWN_H), 0, CL_DEV)
    spare_slots = (CL_DEV - 1) * MOST
    slot_keys = jax.random.split(key_slots, DOCS * HEADS * OWN_H)
    spare_order = jax.vmap(lambda single: jax.random.permutation(single, spare_slots))(slot_keys).astype(jnp.int32)
    spare_order = spare_order.reshape(DOCS, HEADS, OWN_H * spare_slots)
    full_block = jnp.take_along_axis(full_cluster, owner_local, axis=2)
    slot_index = jnp.clip(rank_at - MOST, 0, spare_slots - 1)
    chosen = jnp.take_along_axis(spare_order, owner_local * spare_slots + slot_index, axis=2)
    spare_cluster = chosen // MOST
    spare_cluster = spare_cluster + (spare_cluster >= full_block).astype(jnp.int32)
    local_cluster = jnp.where(rank_at < MOST, full_block, spare_cluster)
    cluster_ids = (owner_local * CL_DEV + local_cluster).astype(jnp.int32)

    def list_one(cluster_row):
        same_cluster = cluster_row[None, :] == cluster_row[:, None]
        position = jnp.sum(same_cluster & (block_ids[None, :] < block_ids[:, None]), axis=1).astype(jnp.int32)
        return jnp.full((CENT, MOST), -1, jnp.int32).at[cluster_row, position].set(block_ids)
    block_lists = lax.map(list_one, cluster_ids.reshape(-1, BLOCKS)).reshape(DOCS, HEADS * CENT, MOST)
    return (cluster_ids, block_lists)


def draw_cluster_of(key, part):
    return route_tables(key)[0]


def draw_block_list(key, part):
    return route_tables(key)[1]


def query_key_pair(base_key):
    key_query = jax.random.fold_in(base_key, 901)
    key_keys = jax.random.fold_in(base_key, 902)
    shape_all = (DOCS, TOKENS, HEADS * HD)
    keys_out = jnp.clip(jax.random.normal(key_keys, shape_all, jnp.float32), -4.0, 4.0)
    queries_out = jnp.clip(jax.random.normal(key_query, shape_all, jnp.float32), -4.0, 4.0)
    return (queries_out, keys_out)


def draw_queries(key, part):
    return query_key_pair(key)[0].astype(jnp.bfloat16)


def draw_keys(key, part):
    return query_key_pair(key)[1].astype(jnp.bfloat16)


def level_of(own_key, extent, shards, least, largest):
    def one(axis_at, parts):
        steps = jax.random.uniform(jax.random.fold_in(jax.random.fold_in(own_key, 6), axis_at), (parts,), jnp.float32, least / len(shards), largest / len(shards))
        return jnp.repeat(jnp.exp(steps), extent[axis_at] // parts).reshape((-1,) + (1,) * (len(extent) - axis_at - 1))

    gain = one(*shards[0])
    for cut in shards[1:]:
        gain = gain * one(*cut)
    return gain


def noise(stream_key, shape, scale, limit, cuts=(), held_as=jnp.bfloat16):
    loudness = level_of(stream_key, shape, cuts, -0.22, 0.18) if cuts else 1.0
    result = jax.random.normal(stream_key, shape, jnp.float32) * scale * loudness
    return jnp.minimum(jnp.maximum(result, -limit), limit).astype(held_as)


def setup_inputs(seed: int = 0) -> dict:
    key_of = jax.random.split(jax.random.key(seed), 8)
    return {
        "queries": draw_queries(jax.random.fold_in(key_of[7], 71), 0),
        "keys": draw_keys(jax.random.fold_in(key_of[7], 71), 0),
        "values": noise(key_of[2], (DOCS, TOKENS, HEADS * HD), 1.0, 4.0, ((0, 2), (1, 16))),
        "cotangent": noise(key_of[3], (DOCS, TOKENS, HEADS * HD), 1.0, 4.0, ((0, 2), (1, 16))),
        "cluster_of": draw_cluster_of(jax.random.fold_in(key_of[7], 71), 0),
        "block_list": draw_block_list(jax.random.fold_in(key_of[7], 71), 0),
        "centroid_sums": noise(key_of[6], (HEADS * CENT, HD), 1.0, 5.0, ((0, 16),), jnp.float32),
    }


decay_rate = 0.99
neg_fill = -1e+30

def attend(q_tiles, k_tiles, v_tiles, d_tiles, positions, present_rows, cluster_rows):
    score_scale = 1.0 / math.sqrt(q_tiles.shape[-1])
    q_wide = q_tiles.astype(jnp.float32)
    k_wide = k_tiles.astype(jnp.float32)
    v_wide = v_tiles.astype(jnp.float32)
    d_wide = d_tiles.astype(jnp.float32)
    scores = jnp.einsum('crd,csd->crs', q_wide, k_wide) * score_scale
    visible = present_rows[:, :, None] & present_rows[:, None, :]
    visible = visible & (positions[:, None, :] <= positions[:, :, None])
    visible = visible & (cluster_rows[:, None, :] == cluster_rows[:, :, None])
    scores = jnp.where(visible, scores, neg_fill)
    row_max = lax.optimization_barrier(jnp.max(scores, axis=-1, keepdims=True))
    raised = jnp.exp(scores - row_max)
    probabilities = jnp.where(visible, raised / lax.optimization_barrier(jnp.sum(raised, axis=-1, keepdims=True)), 0.0)
    weights = lax.optimization_barrier(probabilities.astype(jnp.bfloat16)).astype(jnp.float32)
    out_full = jnp.einsum('crs,csd->crd', weights, v_wide)
    dprobs = jnp.einsum('crd,csd->crs', d_wide, v_wide)
    row_dot = lax.optimization_barrier(jnp.sum(d_wide * out_full, axis=-1, keepdims=True))
    dscores = (probabilities * (dprobs - row_dot) * score_scale).astype(jnp.bfloat16)
    dscores = lax.optimization_barrier(dscores).astype(jnp.float32)
    grad_values = jnp.einsum('crs,crd->csd', weights, d_wide)
    grad_queries = jnp.einsum('crs,csd->crd', dscores, k_wide)
    grad_keys = jnp.einsum('crs,crd->csd', dscores, q_wide)
    return (out_full, grad_queries, grad_keys, grad_values)

def one_head(packed):
    q_head, k_head, v_head, d_head, cluster_row, lists_head = packed
    members = lists_head.reshape(-1)
    present = members >= 0
    picked = jnp.where(present, members, 0).astype(jnp.int32)
    token_offsets = jnp.arange(BLK, dtype=jnp.int32)
    positions = (picked[:, None] * BLK + token_offsets[None, :]).reshape(CENT, MOST * BLK)
    present_rows = jnp.broadcast_to(present[:, None], (CENT * MOST, BLK)).reshape(CENT, MOST * BLK)
    block_cluster = cluster_row[picked]
    cluster_rows = jnp.broadcast_to(block_cluster[:, None], (CENT * MOST, BLK)).reshape(CENT, MOST * BLK)

    def gather_tiles(source):
        return source.reshape(BLOCKS, BLK, HD)[picked].reshape(CENT, MOST * BLK, HD)
    k_tiles = gather_tiles(k_head)
    results = attend(gather_tiles(q_head), k_tiles, gather_tiles(v_head), gather_tiles(d_head), positions, present_rows, cluster_rows)
    key_sum = lax.optimization_barrier(jnp.sum(jnp.where(present_rows[:, :, None], k_tiles.astype(jnp.float32), 0.0), axis=1))
    target = jnp.where(present, members, BLOCKS).astype(jnp.int32)

    def scatter_tiles(tiles_in):
        placed = jnp.zeros((BLOCKS, BLK, HD), jnp.bfloat16)
        placed = placed.at[target].set(tiles_in.astype(jnp.bfloat16).reshape(CENT * MOST, BLK, HD), mode='drop')
        return placed.reshape(TOKENS, HD)
    return (scatter_tiles(results[0]), scatter_tiles(results[1]), scatter_tiles(results[2]), scatter_tiles(results[3]), key_sum)

def reference(queries, keys, values, cotangent, cluster_of, block_list, centroid_sums):

    def split_heads(source):
        return source.reshape(DOCS, TOKENS, HEADS, HD).transpose(0, 2, 1, 3).reshape(DOCS * HEADS, TOKENS, HD)

    def join_heads(source):
        return source.reshape(DOCS, HEADS, TOKENS, HD).transpose(0, 2, 1, 3).reshape(DOCS, TOKENS, HEADS * HD)
    lists_all = block_list.reshape(DOCS * HEADS, CENT, MOST)
    clusters_all = cluster_of.reshape(DOCS * HEADS, BLOCKS)
    results = lax.map(one_head, (split_heads(queries), split_heads(keys), split_heads(values), split_heads(cotangent), clusters_all, lists_all))
    key_sum = lax.optimization_barrier(jnp.sum(results[4].reshape(DOCS, HEADS * CENT, HD), axis=0))
    centroid_next = decay_rate * centroid_sums + (1.0 - decay_rate) * key_sum
    return (join_heads(results[0]), join_heads(results[1]), join_heads(results[2]), join_heads(results[3]), centroid_next)
```

```python
import functools
import math

import jax
import jax.numpy as jnp
from jax import lax
from jax.experimental import pallas as pl
from jax.experimental.pallas import tpu as pltpu
from jax.sharding import PartitionSpec as P

decay_rate = 0.99
neg_fill = -1e30
MESH = pl.DeviceIdType.MESH
PAIR = 2
NT = (((1,), (1,)), ((), ()))
TN = (((0,), (0,)), ((), ()))


def dot_f32(a, b, dims):
    return lax.dot_general(a, b, dims, preferred_element_type=jnp.float32)


def routed_kernel(
    seq_size, dp_size, slot_cap, block_len, head_dim, reach,
    order_ref, rank_ref, first_ref, slots_ref, cent_ref, k_ref, q_ref, v_ref, d_ref,
    out_ref, gq_ref, gk_ref, gv_ref, next_ref,
    k_in, q_in, v_in, d_in, ordered, acc_k, acc_v, made, back, key_rows, sums,
    in_send, in_recv, in_own, back_send, back_recv, back_own, sum_send, sum_recv,
):
    my_dp = lax.axis_index("dp")
    me = lax.axis_index("seq")
    slots = seq_size * slot_cap
    others = (seq_size - 1) * slot_cap
    lead = reach * block_len
    tile = PAIR * block_len
    window = lead + tile
    score_scale = 1.0 / math.sqrt(head_dim)

    barrier = pltpu.get_barrier_semaphore()

    def greet(step, carry):
        pl.semaphore_signal(
            barrier, inc=1, device_id=(my_dp, lax.rem(me + step, seq_size)), device_id_type=MESH
        )
        return carry

    lax.fori_loop(1, seq_size, greet, 0)
    for step in range(1, dp_size):
        pl.semaphore_signal(
            barrier, inc=1, device_id=(lax.rem(my_dp + step, dp_size), me), device_id_type=MESH
        )
    pl.semaphore_wait(barrier, seq_size + dp_size - 2)

    def columns(index):
        return pl.ds(pl.multiple_of(index * head_dim, head_dim), head_dim)

    def rows_of(index):
        return pl.ds(index * slot_cap, slot_cap)

    sources = (k_ref, q_ref, v_ref, d_ref)
    arrived = (k_in, q_in, v_in, d_in)
    for at, source in enumerate(sources):
        pltpu.make_async_copy(
            source.at[:, :, columns(me)], arrived[at].at[rows_of(me)], in_own.at[at]
        ).start()

        def send(step, carry, at=at, source=source):
            target = lax.rem(me + step, seq_size)
            pltpu.make_async_remote_copy(
                src_ref=source.at[:, :, columns(target)],
                dst_ref=arrived[at].at[rows_of(me)],
                send_sem=in_send.at[at],
                recv_sem=in_recv.at[at],
                device_id=(my_dp, target),
                device_id_type=MESH,
            ).start()
            return carry

        lax.fori_loop(1, seq_size, send, 0)

    ordered[:, :lead, :] = jnp.zeros((4, lead, head_dim), jnp.bfloat16)
    acc_k[...] = jnp.zeros_like(acc_k)
    acc_v[...] = jnp.zeros_like(acc_v)

    def bytes_of(at):
        return arrived[at].at[pl.ds(0, others)]

    for at, source in enumerate(sources):
        part = bytes_of(at)
        pltpu.make_async_copy(part, part, in_recv.at[at]).wait()
        pltpu.make_async_copy(
            source.at[:, :, columns(me)], arrived[at].at[rows_of(me)], in_own.at[at]
        ).wait()

        def place(spot, carry, at=at):
            rows = pl.ds(pl.multiple_of(lead + spot * block_len, block_len), block_len)
            ordered[at, rows, :] = arrived[at][order_ref[spot]]
            if at == 0:
                key_rows[pl.ds(spot, 1), :] = jnp.sum(
                    k_in[spot].astype(jnp.float32), axis=0, keepdims=True
                )
            return carry

        lax.fori_loop(0, slots, place, 0)
        if at == 0:
            groups = slots_ref.shape[0]
            spots = lax.broadcasted_iota(jnp.int32, (groups, slots), 1)
            member = jnp.zeros((groups, slots), jnp.float32)
            for one in range(slots_ref.shape[1]):
                member += jnp.where(slots_ref[:, one : one + 1] == spots, 1.0, 0.0)
            sums[my_dp] = lax.dot_general(
                member, key_rows[...], (((1,), (0,)), ((), ())),
                precision=lax.Precision.HIGHEST, preferred_element_type=jnp.float32,
            )
            for step in range(1, dp_size):
                target = lax.rem(my_dp + step, dp_size)
                pltpu.make_async_remote_copy(
                    src_ref=sums.at[my_dp],
                    dst_ref=sums.at[my_dp],
                    send_sem=sum_send.at[step],
                    recv_sem=sum_recv.at[step],
                    device_id=(target, me),
                    device_id_type=MESH,
                ).start()

    row_at = lax.broadcasted_iota(jnp.int32, (tile, window), 0)
    col_at = lax.broadcasted_iota(jnp.int32, (tile, window), 1)
    below = col_at <= row_at + lead
    row_one = lax.broadcasted_iota(jnp.int32, (tile, 1), 0)

    def attend(index, carry):
        start = pl.multiple_of(index * tile, tile)
        own = pl.ds(pl.multiple_of(start + lead, block_len), tile)
        near = pl.ds(start, window)
        k = ordered[0, near, :]
        q = ordered[1, own, :]
        v = ordered[2, near, :]
        g = ordered[3, own, :]
        low = jnp.zeros((tile, 1), jnp.int32)
        for one in range(PAIR):
            edge = lead + (first_ref[index * PAIR + one] - index * PAIR) * block_len
            low = jnp.where(row_one >= one * block_len, edge, low)
        visible = below & (col_at >= low)
        scores = jnp.where(visible, dot_f32(q, k, NT) * score_scale, neg_fill)
        raised = jnp.exp(scores - jnp.max(scores, axis=-1, keepdims=True))
        probs = raised / jnp.sum(raised, axis=-1, keepdims=True)
        weights = probs.astype(jnp.bfloat16)
        out_full = dot_f32(weights, v, (((1,), (0,)), ((), ())))
        dprobs = dot_f32(g, v, NT)
        row_dot = jnp.sum(g.astype(jnp.float32) * out_full, axis=-1, keepdims=True)
        dscores = (probs * (dprobs - row_dot) * score_scale).astype(jnp.bfloat16)
        here = pl.ds(index * PAIR, PAIR)
        tiled = (PAIR, block_len, head_dim)
        grad_q = dot_f32(dscores, k, (((1,), (0,)), ((), ())))
        made[0, here] = out_full.astype(jnp.bfloat16).reshape(tiled)
        made[1, here] = grad_q.astype(jnp.bfloat16).reshape(tiled)
        acc_k[near, :] += dot_f32(dscores, q, TN)
        acc_v[near, :] += dot_f32(weights, g, TN)
        return carry

    lax.fori_loop(0, slots // PAIR, attend, 0)
    made[2] = acc_k[lead:, :].astype(jnp.bfloat16).reshape(slots, block_len, head_dim)
    made[3] = acc_v[lead:, :].astype(jnp.bfloat16).reshape(slots, block_len, head_dim)

    results = (out_ref, gq_ref, gk_ref, gv_ref)
    for at, result in enumerate(results):

        def settle(spot, carry, at=at):
            back[at, spot] = made[at, rank_ref[spot]]
            return carry

        lax.fori_loop(0, slots, settle, 0)
        pltpu.make_async_copy(
            back.at[at, rows_of(me)], result.at[:, :, columns(me)], back_own.at[at]
        ).start()

        def give(step, carry, at=at, result=result):
            target = lax.rem(me + step, seq_size)
            pltpu.make_async_remote_copy(
                src_ref=back.at[at, rows_of(target)],
                dst_ref=result.at[:, :, columns(me)],
                send_sem=back_send.at[at],
                recv_sem=back_recv.at[at],
                device_id=(my_dp, target),
                device_id_type=MESH,
            ).start()
            return carry

        lax.fori_loop(1, seq_size, give, 0)

    for step in range(1, dp_size):
        source_dp = lax.rem(my_dp - step + dp_size, dp_size)
        swap = pltpu.make_async_remote_copy(
            src_ref=sums.at[my_dp],
            dst_ref=sums.at[source_dp],
            send_sem=sum_send.at[step],
            recv_sem=sum_recv.at[step],
            device_id=(lax.rem(my_dp + step, dp_size), me),
            device_id_type=MESH,
        )
        swap.wait_recv()
        swap.wait_send()
    total = sums[0]
    for one in range(1, dp_size):
        total = total + sums[one]
    next_ref[...] = decay_rate * cent_ref[...] + (1.0 - decay_rate) * total

    for at, result in enumerate(results):
        moved = bytes_of(at)
        pltpu.make_async_copy(moved, moved, in_send.at[at]).wait()
        pltpu.make_async_copy(moved, moved, back_recv.at[at]).wait()
        pltpu.make_async_copy(moved, moved, back_send.at[at]).wait()
        pltpu.make_async_copy(
            back.at[at, rows_of(me)], result.at[:, :, columns(me)], back_own.at[at]
        ).wait()


def per_device(queries, keys, values, cotangent, cluster_of, block_list, centroid_sums):
    seq_size = lax.axis_size("seq")
    dp_size = lax.axis_size("dp")
    head_count = cluster_of.shape[1]
    block_count = cluster_of.shape[2]
    token_count = queries.shape[1]
    block_len = token_count // block_count
    head_dim = centroid_sums.shape[1]
    groups_here = block_list.shape[1]
    cluster_cap = block_list.shape[2]
    owner_count = seq_size // head_count
    slot_cap = min(block_count, max(1, 2 * block_count // owner_count))
    slots = seq_size * slot_cap
    reach = -(-(cluster_cap - 1) // PAIR) * PAIR
    members = block_list[0]
    present = members >= 0
    if owner_count == 1:
        slot_table = members

        def pack(source):
            return source.reshape(block_count, block_len, seq_size * head_dim)

        def unpack(returned):
            return returned.reshape(1, token_count, head_count * head_dim)

    else:
        owner_local = cluster_of[0] // groups_here
        earlier = jnp.arange(block_count)[:, None] < jnp.arange(block_count)[None, :]
        same_owner = owner_local[:, :, None] == owner_local[:, None, :]
        slot_of = jnp.sum(same_owner & earlier[None], axis=1)
        selector = owner_local[:, None, None, :] == jnp.arange(owner_count)[None, :, None, None]
        selector = selector & (slot_of[:, None, None, :] == jnp.arange(slot_cap)[None, None, :, None])
        selector = selector.astype(jnp.bfloat16)

        def pack(source):
            blocks_in = source[0].reshape(block_count, block_len, head_count, head_dim)
            outgoing = jnp.einsum(
                "hlcj,jthd->cthld", selector, blocks_in, preferred_element_type=jnp.float32
            )
            return outgoing.astype(jnp.bfloat16).reshape(slot_cap, block_len, seq_size * head_dim)

        def unpack(returned):
            arranged = returned.reshape(slot_cap, block_len, head_count, owner_count, head_dim)
            gathered = jnp.einsum(
                "hlcj,cthld->jthd", selector, arranged, preferred_element_type=jnp.float32
            )
            return gathered.astype(jnp.bfloat16).reshape(1, token_count, head_count * head_dim)

        flat = members.reshape(-1)
        source_dev = jnp.where(flat >= 0, flat // block_count, -1)
        before = (
            (flat >= 0)[None, :]
            & (source_dev[None, :] == source_dev[:, None])
            & (flat[None, :] < flat[:, None])
        )
        slot_at = jnp.sum(before, axis=1)
        slot_table = jnp.where(flat >= 0, source_dev * slot_cap + slot_at, -1)
        slot_table = slot_table.reshape(members.shape).astype(jnp.int32)

    spots = jnp.arange(slots, dtype=jnp.int32)
    holds = slot_table.reshape(-1)[:, None] == spots[None, :]
    place = jnp.arange(holds.shape[0], dtype=jnp.int32)
    place_of = jnp.sum(jnp.where(holds, place[:, None] + 1, 0), axis=0)
    place_of = jnp.where(place_of > 0, place_of - 1, (groups_here + spots) * cluster_cap)
    rank = jnp.sum(place_of[None, :] < place_of[:, None], axis=1).astype(jnp.int32)
    cluster_at = place_of // cluster_cap
    first_slot = jnp.sum(cluster_at[None, :] < cluster_at[:, None], axis=1).astype(jnp.int32)
    at_rank = rank[None, :] == spots[:, None]
    order = jnp.sum(jnp.where(at_rank, spots[None, :], 0), axis=1).astype(jnp.int32)
    first = jnp.sum(jnp.where(at_rank, first_slot[None, :], 0), axis=1).astype(jnp.int32)

    lead = reach * block_len
    any_spec = pl.BlockSpec(memory_space=pl.ANY)
    smem_spec = pl.BlockSpec(memory_space=pltpu.SMEM)
    vmem_spec = pl.BlockSpec(memory_space=pltpu.VMEM)
    packed_shape = jax.ShapeDtypeStruct((slot_cap, block_len, seq_size * head_dim), jnp.bfloat16)
    results = pl.pallas_call(
        functools.partial(
            routed_kernel, seq_size, dp_size, slot_cap, block_len, head_dim, reach
        ),
        out_shape=(packed_shape,) * 4
        + (jax.ShapeDtypeStruct((groups_here, head_dim), jnp.float32),),
        in_specs=[smem_spec] * 3 + [vmem_spec] * 2 + [any_spec] * 4,
        out_specs=(any_spec,) * 4 + (vmem_spec,),
        scratch_shapes=[
            *[pltpu.VMEM((slots, block_len, head_dim), jnp.bfloat16)] * 4,
            pltpu.VMEM((4, lead + slots * block_len, head_dim), jnp.bfloat16),
            pltpu.VMEM((lead + slots * block_len, head_dim), jnp.float32),
            pltpu.VMEM((lead + slots * block_len, head_dim), jnp.float32),
            pltpu.VMEM((4, slots, block_len, head_dim), jnp.bfloat16),
            pltpu.VMEM((4, slots, block_len, head_dim), jnp.bfloat16),
            pltpu.VMEM((slots, head_dim), jnp.float32),
            pltpu.VMEM((dp_size, groups_here, head_dim), jnp.float32),
        ]
        + [pltpu.SemaphoreType.DMA((4,))] * 6
        + [pltpu.SemaphoreType.DMA((dp_size,))] * 2,
        compiler_params=pltpu.CompilerParams(
            collective_id=0, has_side_effects=True, vmem_limit_bytes=48 * 1024 * 1024
        ),
    )(
        order, rank, first, slot_table, centroid_sums,
        pack(keys), pack(queries), pack(values), pack(cotangent),
    )
    return tuple(unpack(item) for item in results[:4]) + (results[4],)


def solution(mesh):
    in_specs = (
        P("dp", "seq", None),
        P("dp", "seq", None),
        P("dp", "seq", None),
        P("dp", "seq", None),
        P("dp", None, "seq"),
        P("dp", "seq", None),
        P("seq", None),
    )
    out_specs = (
        P("dp", "seq", None),
        P("dp", "seq", None),
        P("dp", "seq", None),
        P("dp", "seq", None),
        P("seq", None),
    )
    return jax.shard_map(
        per_device, mesh=mesh, in_specs=in_specs, out_specs=out_specs, check_vma=False
    )
```

```python
import functools
import math

import jax
import jax.numpy as jnp
from jax import lax
from jax.experimental import pallas as pl
from jax.experimental.pallas import tpu as pltpu
from jax.sharding import PartitionSpec as P

decay_rate = 0.99
neg_fill = -1e30
MESH = pl.DeviceIdType.MESH
PAIR = 2
NT = (((1,), (1,)), ((), ()))
TN = (((0,), (0,)), ((), ()))
NN = (((1,), (0,)), ((), ()))


def dot_f32(a, b, dims):
    return lax.dot_general(a, b, dims, preferred_element_type=jnp.float32)


def routed_kernel(
    seq_size, dp_size, slot_cap, block_len, head_dim, reach,
    order_ref, rank_ref, first_ref, slots_ref, cent_ref, k_ref, q_ref, v_ref, d_ref,
    out_ref, gq_ref, gk_ref, gv_ref, next_ref,
    k_in, q_in, v_in, d_in, ordered, probs_at, full_at, acc_k, acc_v, made, back, key_rows, sums,
    in_send, in_recv, in_own, back_send, back_recv, back_own, sum_send, sum_recv,
):
    my_dp = lax.axis_index("dp")
    me = lax.axis_index("seq")
    slots = seq_size * slot_cap
    others = (seq_size - 1) * slot_cap
    lead = reach * block_len
    tile = PAIR * block_len
    window = lead + tile
    score_scale = 1.0 / math.sqrt(head_dim)

    barrier = pltpu.get_barrier_semaphore()

    def greet(step, carry):
        pl.semaphore_signal(
            barrier, inc=1, device_id=(my_dp, lax.rem(me + step, seq_size)), device_id_type=MESH
        )
        return carry

    lax.fori_loop(1, seq_size, greet, 0)
    for step in range(1, dp_size):
        pl.semaphore_signal(
            barrier, inc=1, device_id=(lax.rem(my_dp + step, dp_size), me), device_id_type=MESH
        )
    pl.semaphore_wait(barrier, seq_size + dp_size - 2)

    def columns(index):
        return pl.ds(pl.multiple_of(index * head_dim, head_dim), head_dim)

    def rows_of(index):
        return pl.ds(index * slot_cap, slot_cap)

    sources = (k_ref, q_ref, v_ref, d_ref)
    arrived = (k_in, q_in, v_in, d_in)
    for at, source in enumerate(sources):
        pltpu.make_async_copy(
            source.at[:, :, columns(me)], arrived[at].at[rows_of(me)], in_own.at[at]
        ).start()

        def send(step, carry, at=at, source=source):
            target = lax.rem(me + step, seq_size)
            pltpu.make_async_remote_copy(
                src_ref=source.at[:, :, columns(target)],
                dst_ref=arrived[at].at[rows_of(me)],
                send_sem=in_send.at[at],
                recv_sem=in_recv.at[at],
                device_id=(my_dp, target),
                device_id_type=MESH,
            ).start()
            return carry

        lax.fori_loop(1, seq_size, send, 0)

    ordered[:, :lead, :] = jnp.zeros((4, lead, head_dim), jnp.bfloat16)
    acc_k[...] = jnp.zeros_like(acc_k)
    acc_v[...] = jnp.zeros_like(acc_v)

    def bytes_of(at):
        return arrived[at].at[pl.ds(0, others)]

    def collect(at):
        part = bytes_of(at)
        pltpu.make_async_copy(part, part, in_recv.at[at]).wait()
        pltpu.make_async_copy(
            sources[at].at[:, :, columns(me)], arrived[at].at[rows_of(me)], in_own.at[at]
        ).wait()

        def place(spot, carry):
            rows = pl.ds(pl.multiple_of(lead + spot * block_len, block_len), block_len)
            ordered[at, rows, :] = arrived[at][order_ref[spot]]
            return carry

        lax.fori_loop(0, slots, place, 0, unroll=4)

    results = (out_ref, gq_ref, gk_ref, gv_ref)

    def give_back(at):
        result = results[at]

        def settle(spot, carry):
            back[at, spot] = made[at, rank_ref[spot]]
            return carry

        lax.fori_loop(0, slots, settle, 0, unroll=4)
        pltpu.make_async_copy(
            back.at[at, rows_of(me)], result.at[:, :, columns(me)], back_own.at[at]
        ).start()

        def give(step, carry):
            target = lax.rem(me + step, seq_size)
            pltpu.make_async_remote_copy(
                src_ref=back.at[at, rows_of(target)],
                dst_ref=result.at[:, :, columns(me)],
                send_sem=back_send.at[at],
                recv_sem=back_recv.at[at],
                device_id=(my_dp, target),
                device_id_type=MESH,
            ).start()
            return carry

        lax.fori_loop(1, seq_size, give, 0)

    row_at = lax.broadcasted_iota(jnp.int32, (tile, window), 0)
    col_at = lax.broadcasted_iota(jnp.int32, (tile, window), 1)
    row_one = lax.broadcasted_iota(jnp.int32, (tile, 1), 0)
    tiled = (PAIR, block_len, head_dim)

    def spans(index):
        start = pl.multiple_of(index * tile, tile)
        own = pl.ds(pl.multiple_of(start + lead, block_len), tile)
        return own, pl.ds(start, window), pl.ds(index * PAIR, PAIR)

    def forward(index, carry):
        own, near, here = spans(index)
        low = jnp.zeros((tile, 1), jnp.int32)
        for one in range(PAIR):
            edge = lead + (first_ref[index * PAIR + one] - index * PAIR) * block_len
            low = jnp.where(row_one >= one * block_len, edge, low)
        visible = (col_at <= row_at + lead) & (col_at >= low)
        scores = dot_f32(ordered[1, own, :], ordered[0, near, :], NT) * score_scale
        scores = jnp.where(visible, scores, neg_fill)
        raised = jnp.exp(scores - jnp.max(scores, axis=-1, keepdims=True))
        probs = raised / jnp.sum(raised, axis=-1, keepdims=True)
        out_full = dot_f32(probs.astype(jnp.bfloat16), ordered[2, near, :], NN)
        probs_at[index] = probs
        full_at[index] = out_full
        made[0, here] = out_full.astype(jnp.bfloat16).reshape(tiled)
        return carry

    def backward(index, carry):
        own, near, here = spans(index)
        k = ordered[0, near, :]
        q = ordered[1, own, :]
        g = ordered[3, own, :]
        probs = probs_at[index]
        dprobs = dot_f32(g, ordered[2, near, :], NT)
        row_dot = jnp.sum(g.astype(jnp.float32) * full_at[index], axis=-1, keepdims=True)
        dscores = (probs * (dprobs - row_dot) * score_scale).astype(jnp.bfloat16)
        made[1, here] = dot_f32(dscores, k, NN).astype(jnp.bfloat16).reshape(tiled)
        acc_k[near, :] += dot_f32(dscores, q, TN)
        acc_v[near, :] += dot_f32(probs.astype(jnp.bfloat16), g, TN)
        return carry

    collect(0)
    collect(1)
    collect(2)
    lax.fori_loop(0, slots // PAIR, forward, 0, unroll=4)
    give_back(0)
    collect(3)
    lax.fori_loop(0, slots // PAIR, backward, 0, unroll=2)
    give_back(1)
    made[2] = acc_k[lead:, :].astype(jnp.bfloat16).reshape(slots, block_len, head_dim)
    give_back(2)
    made[3] = acc_v[lead:, :].astype(jnp.bfloat16).reshape(slots, block_len, head_dim)
    give_back(3)

    def add_keys(spot, carry):
        key_rows[pl.ds(spot, 1), :] = jnp.sum(
            k_in[spot].astype(jnp.float32), axis=0, keepdims=True
        )
        return carry

    lax.fori_loop(0, slots, add_keys, 0)
    groups = slots_ref.shape[0]
    spots = lax.broadcasted_iota(jnp.int32, (groups, slots), 1)
    member = jnp.zeros((groups, slots), jnp.float32)
    for one in range(slots_ref.shape[1]):
        member += jnp.where(slots_ref[:, one : one + 1] == spots, 1.0, 0.0)
    sums[my_dp] = lax.dot_general(
        member, key_rows[...], NN,
        precision=lax.Precision.HIGHEST, preferred_element_type=jnp.float32,
    )
    for step in range(1, dp_size):
        target = lax.rem(my_dp + step, dp_size)
        pltpu.make_async_remote_copy(
            src_ref=sums.at[my_dp],
            dst_ref=sums.at[my_dp],
            send_sem=sum_send.at[step],
            recv_sem=sum_recv.at[step],
            device_id=(target, me),
            device_id_type=MESH,
        ).start()

    for step in range(1, dp_size):
        source_dp = lax.rem(my_dp - step + dp_size, dp_size)
        swap = pltpu.make_async_remote_copy(
            src_ref=sums.at[my_dp],
            dst_ref=sums.at[source_dp],
            send_sem=sum_send.at[step],
            recv_sem=sum_recv.at[step],
            device_id=(lax.rem(my_dp + step, dp_size), me),
            device_id_type=MESH,
        )
        swap.wait_recv()
        swap.wait_send()
    total = sums[0]
    for one in range(1, dp_size):
        total = total + sums[one]
    next_ref[...] = decay_rate * cent_ref[...] + (1.0 - decay_rate) * total

    for at, result in enumerate(results):
        moved = bytes_of(at)
        pltpu.make_async_copy(moved, moved, in_send.at[at]).wait()
        pltpu.make_async_copy(moved, moved, back_recv.at[at]).wait()
        pltpu.make_async_copy(moved, moved, back_send.at[at]).wait()
        pltpu.make_async_copy(
            back.at[at, rows_of(me)], result.at[:, :, columns(me)], back_own.at[at]
        ).wait()


def settle_kernel(*refs):
    held, results, done = refs[:5], refs[5:10], refs[10]
    copies = [
        pltpu.make_async_copy(source, result, done.at[at])
        for at, (source, result) in enumerate(zip(held, results))
    ]
    for copy in copies:
        copy.start()
    for copy in copies:
        copy.wait()


def per_device(queries, keys, values, cotangent, cluster_of, block_list, centroid_sums):
    seq_size = lax.axis_size("seq")
    dp_size = lax.axis_size("dp")
    head_count = cluster_of.shape[1]
    block_count = cluster_of.shape[2]
    token_count = queries.shape[1]
    block_len = token_count // block_count
    head_dim = centroid_sums.shape[1]
    groups_here = block_list.shape[1]
    cluster_cap = block_list.shape[2]
    owner_count = seq_size // head_count
    slot_cap = min(block_count, max(1, 2 * block_count // owner_count))
    slots = seq_size * slot_cap
    reach = -(-(cluster_cap - 1) // PAIR) * PAIR
    members = block_list[0]
    present = members >= 0
    if owner_count == 1:
        slot_table = members

        def pack(source):
            return source.reshape(block_count, block_len, seq_size * head_dim)

        def unpack(returned):
            return returned.reshape(1, token_count, head_count * head_dim)

    else:
        owner_local = cluster_of[0] // groups_here
        earlier = jnp.arange(block_count)[:, None] < jnp.arange(block_count)[None, :]
        same_owner = owner_local[:, :, None] == owner_local[:, None, :]
        slot_of = jnp.sum(same_owner & earlier[None], axis=1)
        selector = owner_local[:, None, None, :] == jnp.arange(owner_count)[None, :, None, None]
        selector = selector & (slot_of[:, None, None, :] == jnp.arange(slot_cap)[None, None, :, None])
        selector = selector.astype(jnp.bfloat16)

        def pack(source):
            blocks_in = source[0].reshape(block_count, block_len, head_count, head_dim)
            outgoing = jnp.einsum(
                "hlcj,jthd->cthld", selector, blocks_in, preferred_element_type=jnp.float32
            )
            return outgoing.astype(jnp.bfloat16).reshape(slot_cap, block_len, seq_size * head_dim)

        def unpack(returned):
            arranged = returned.reshape(slot_cap, block_len, head_count, owner_count, head_dim)
            gathered = jnp.einsum(
                "hlcj,cthld->jthd", selector, arranged, preferred_element_type=jnp.float32
            )
            return gathered.astype(jnp.bfloat16).reshape(1, token_count, head_count * head_dim)

        flat = members.reshape(-1)
        source_dev = jnp.where(flat >= 0, flat // block_count, -1)
        before = (
            (flat >= 0)[None, :]
            & (source_dev[None, :] == source_dev[:, None])
            & (flat[None, :] < flat[:, None])
        )
        slot_at = jnp.sum(before, axis=1)
        slot_table = jnp.where(flat >= 0, source_dev * slot_cap + slot_at, -1)
        slot_table = slot_table.reshape(members.shape).astype(jnp.int32)

    spots = jnp.arange(slots, dtype=jnp.int32)
    holds = slot_table.reshape(-1)[:, None] == spots[None, :]
    place = jnp.arange(holds.shape[0], dtype=jnp.int32)
    place_of = jnp.sum(jnp.where(holds, place[:, None] + 1, 0), axis=0)
    place_of = jnp.where(place_of > 0, place_of - 1, (groups_here + spots) * cluster_cap)
    rank = jnp.sum(place_of[None, :] < place_of[:, None], axis=1).astype(jnp.int32)
    cluster_at = place_of // cluster_cap
    first_slot = jnp.sum(cluster_at[None, :] < cluster_at[:, None], axis=1).astype(jnp.int32)
    at_rank = rank[None, :] == spots[:, None]
    order = jnp.sum(jnp.where(at_rank, spots[None, :], 0), axis=1).astype(jnp.int32)
    first = jnp.sum(jnp.where(at_rank, first_slot[None, :], 0), axis=1).astype(jnp.int32)

    lead = reach * block_len
    any_spec = pl.BlockSpec(memory_space=pl.ANY)
    smem_spec = pl.BlockSpec(memory_space=pltpu.SMEM)
    vmem_spec = pl.BlockSpec(memory_space=pltpu.VMEM)
    packed_shape = jax.ShapeDtypeStruct((slot_cap, block_len, seq_size * head_dim), jnp.bfloat16)
    results = pl.pallas_call(
        functools.partial(
            routed_kernel, seq_size, dp_size, slot_cap, block_len, head_dim, reach
        ),
        out_shape=(packed_shape,) * 4
        + (jax.ShapeDtypeStruct((groups_here, head_dim), jnp.float32),),
        in_specs=[smem_spec] * 3 + [vmem_spec] * 2 + [pl.BlockSpec(memory_space=pltpu.HBM)] * 4,
        out_specs=(any_spec,) * 4 + (vmem_spec,),
        scratch_shapes=[
            *[pltpu.VMEM((slots, block_len, head_dim), jnp.bfloat16)] * 4,
            pltpu.VMEM((4, lead + slots * block_len, head_dim), jnp.bfloat16),
            pltpu.VMEM((slots // PAIR, PAIR * block_len, lead + PAIR * block_len), jnp.float32),
            pltpu.VMEM((slots // PAIR, PAIR * block_len, head_dim), jnp.float32),
            pltpu.VMEM((lead + slots * block_len, head_dim), jnp.float32),
            pltpu.VMEM((lead + slots * block_len, head_dim), jnp.float32),
            pltpu.VMEM((4, slots, block_len, head_dim), jnp.bfloat16),
            pltpu.VMEM((4, slots, block_len, head_dim), jnp.bfloat16),
            pltpu.VMEM((slots, head_dim), jnp.float32),
            pltpu.VMEM((dp_size, groups_here, head_dim), jnp.float32),
        ]
        + [pltpu.SemaphoreType.DMA((4,))] * 6
        + [pltpu.SemaphoreType.DMA((dp_size,))] * 2,
        compiler_params=pltpu.CompilerParams(
            collective_id=0, has_side_effects=True, vmem_limit_bytes=60 * 1024 * 1024
        ),
    )(
        order, rank, first, slot_table, centroid_sums,
        pack(keys), pack(queries), pack(values), pack(cotangent),
    )
    if owner_count == 1:
        results = pl.pallas_call(
            settle_kernel,
            out_shape=tuple(jax.ShapeDtypeStruct(item.shape, item.dtype) for item in results),
            in_specs=[any_spec] * 5,
            out_specs=(any_spec,) * 5,
            scratch_shapes=[pltpu.SemaphoreType.DMA((5,))],
            compiler_params=pltpu.CompilerParams(vmem_limit_bytes=60 * 1024 * 1024),
        )(*results)
    return tuple(unpack(item) for item in results[:4]) + (results[4],)


def solution(mesh):
    in_specs = (
        P("dp", "seq", None),
        P("dp", "seq", None),
        P("dp", "seq", None),
        P("dp", "seq", None),
        P("dp", None, "seq"),
        P("dp", "seq", None),
        P("seq", None),
    )
    out_specs = (
        P("dp", "seq", None),
        P("dp", "seq", None),
        P("dp", "seq", None),
        P("dp", "seq", None),
        P("seq", None),
    )
    return jax.shard_map(
        per_device, mesh=mesh, in_specs=in_specs, out_specs=out_specs, check_vma=False
    )
```

```python
import functools
import math

import jax
import jax.numpy as jnp
from jax import lax
from jax.experimental import pallas as pl
from jax.experimental.pallas import tpu as pltpu
from jax.sharding import PartitionSpec as P

decay_rate = 0.99
neg_fill = -1e30
MESH = pl.DeviceIdType.MESH
PAIR = 2
NT = (((1,), (1,)), ((), ()))
TN = (((0,), (0,)), ((), ()))
NN = (((1,), (0,)), ((), ()))


def dot_f32(a, b, dims):
    return lax.dot_general(a, b, dims, preferred_element_type=jnp.float32)


def routed_kernel(
    seq_size, dp_size, slot_cap, block_len, head_dim, reach,
    order_ref, rank_ref, first_ref, slots_ref, cent_ref, k_ref, q_ref, v_ref, d_ref,
    out_ref, gq_ref, gk_ref, gv_ref, next_ref,
    k_in, q_in, v_in, d_in, ordered, probs_at, full_at, acc_k, acc_v, made, back, key_rows, sums,
    in_send, in_recv, in_own, back_send, back_recv, back_own, sum_send, sum_recv,
):
    my_dp = lax.axis_index("dp")
    me = lax.axis_index("seq")
    slots = seq_size * slot_cap
    others = (seq_size - 1) * slot_cap
    lead = reach * block_len
    tile = PAIR * block_len
    window = lead + tile
    score_scale = 1.0 / math.sqrt(head_dim)

    barrier = pltpu.get_barrier_semaphore()

    def greet(step, carry):
        pl.semaphore_signal(
            barrier, inc=1, device_id=(my_dp, lax.rem(me + step, seq_size)), device_id_type=MESH
        )
        return carry

    lax.fori_loop(1, seq_size, greet, 0)
    for step in range(1, dp_size):
        pl.semaphore_signal(
            barrier, inc=1, device_id=(lax.rem(my_dp + step, dp_size), me), device_id_type=MESH
        )
    pl.semaphore_wait(barrier, seq_size + dp_size - 2)

    def partner(step):
        if seq_size & (seq_size - 1):
            return lax.rem(me + step, seq_size)
        odd = lax.rem(step, 2)
        offset = odd * (seq_size // 2) + step // 2
        target = 0
        for bit in range(seq_size.bit_length() - 1):
            mine = lax.rem(me // (1 << bit), 2)
            other = lax.rem(offset // (1 << bit), 2)
            target = target + (mine + other - 2 * mine * other) * (1 << bit)
        return target

    def columns(index):
        return pl.ds(pl.multiple_of(index * head_dim, head_dim), head_dim)

    def rows_of(index):
        return pl.ds(index * slot_cap, slot_cap)

    sources = (k_ref, q_ref, v_ref, d_ref)
    arrived = (k_in, q_in, v_in, d_in)
    for at, source in enumerate(sources):
        pltpu.make_async_copy(
            source.at[:, :, columns(me)], arrived[at].at[rows_of(me)], in_own.at[at]
        ).start()

        def send(step, carry, at=at, source=source):
            target = partner(step)
            pltpu.make_async_remote_copy(
                src_ref=source.at[:, :, columns(target)],
                dst_ref=arrived[at].at[rows_of(me)],
                send_sem=in_send.at[at],
                recv_sem=in_recv.at[at],
                device_id=(my_dp, target),
                device_id_type=MESH,
            ).start()
            return carry

        lax.fori_loop(1, seq_size, send, 0)

    ordered[:, :lead, :] = jnp.zeros((4, lead, head_dim), jnp.bfloat16)
    acc_k[...] = jnp.zeros_like(acc_k)
    acc_v[...] = jnp.zeros_like(acc_v)

    def bytes_of(at):
        return arrived[at].at[pl.ds(0, others)]

    def collect(at):
        part = bytes_of(at)
        pltpu.make_async_copy(part, part, in_recv.at[at]).wait()
        pltpu.make_async_copy(
            sources[at].at[:, :, columns(me)], arrived[at].at[rows_of(me)], in_own.at[at]
        ).wait()

        def place(spot, carry):
            rows = pl.ds(pl.multiple_of(lead + spot * block_len, block_len), block_len)
            ordered[at, rows, :] = arrived[at][order_ref[spot]]
            return carry

        lax.fori_loop(0, slots, place, 0, unroll=4)

    results = (out_ref, gq_ref, gk_ref, gv_ref)

    def give_back(at):
        result = results[at]

        def settle(spot, carry):
            back[at, spot] = made[at, rank_ref[spot]]
            return carry

        lax.fori_loop(0, slots, settle, 0, unroll=4)
        pltpu.make_async_copy(
            back.at[at, rows_of(me)], result.at[:, :, columns(me)], back_own.at[at]
        ).start()

        def give(step, carry):
            target = partner(step)
            pltpu.make_async_remote_copy(
                src_ref=back.at[at, rows_of(target)],
                dst_ref=result.at[:, :, columns(me)],
                send_sem=back_send.at[at],
                recv_sem=back_recv.at[at],
                device_id=(my_dp, target),
                device_id_type=MESH,
            ).start()
            return carry

        lax.fori_loop(1, seq_size, give, 0)

    row_at = lax.broadcasted_iota(jnp.int32, (tile, window), 0)
    col_at = lax.broadcasted_iota(jnp.int32, (tile, window), 1)
    row_one = lax.broadcasted_iota(jnp.int32, (tile, 1), 0)
    tiled = (PAIR, block_len, head_dim)

    def spans(index):
        start = pl.multiple_of(index * tile, tile)
        own = pl.ds(pl.multiple_of(start + lead, block_len), tile)
        return own, pl.ds(start, window), pl.ds(index * PAIR, PAIR)

    def forward(index, carry):
        own, near, here = spans(index)
        low = jnp.zeros((tile, 1), jnp.int32)
        for one in range(PAIR):
            edge = lead + (first_ref[index * PAIR + one] - index * PAIR) * block_len
            low = jnp.where(row_one >= one * block_len, edge, low)
        visible = (col_at <= row_at + lead) & (col_at >= low)
        scores = dot_f32(ordered[1, own, :], ordered[0, near, :], NT) * score_scale
        scores = jnp.where(visible, scores, neg_fill)
        raised = jnp.exp(scores - jnp.max(scores, axis=-1, keepdims=True))
        probs = raised / jnp.sum(raised, axis=-1, keepdims=True)
        out_full = dot_f32(probs.astype(jnp.bfloat16), ordered[2, near, :], NN)
        probs_at[index] = probs
        full_at[index] = out_full
        made[0, here] = out_full.astype(jnp.bfloat16).reshape(tiled)
        return carry

    def backward(index, carry):
        own, near, here = spans(index)
        k = ordered[0, near, :]
        q = ordered[1, own, :]
        g = ordered[3, own, :]
        probs = probs_at[index]
        dprobs = dot_f32(g, ordered[2, near, :], NT)
        row_dot = jnp.sum(g.astype(jnp.float32) * full_at[index], axis=-1, keepdims=True)
        dscores = (probs * (dprobs - row_dot) * score_scale).astype(jnp.bfloat16)
        made[1, here] = dot_f32(dscores, k, NN).astype(jnp.bfloat16).reshape(tiled)
        acc_k[near, :] += dot_f32(dscores, q, TN)
        acc_v[near, :] += dot_f32(probs.astype(jnp.bfloat16), g, TN)
        return carry

    collect(0)
    collect(1)
    collect(2)
    lax.fori_loop(0, slots // PAIR, forward, 0, unroll=4)
    give_back(0)
    collect(3)
    lax.fori_loop(0, slots // PAIR, backward, 0, unroll=2)
    give_back(1)
    made[2] = acc_k[lead:, :].astype(jnp.bfloat16).reshape(slots, block_len, head_dim)
    give_back(2)
    made[3] = acc_v[lead:, :].astype(jnp.bfloat16).reshape(slots, block_len, head_dim)
    give_back(3)

    def add_keys(spot, carry):
        key_rows[pl.ds(spot, 1), :] = jnp.sum(
            k_in[spot].astype(jnp.float32), axis=0, keepdims=True
        )
        return carry

    lax.fori_loop(0, slots, add_keys, 0)
    groups = slots_ref.shape[0]
    spots = lax.broadcasted_iota(jnp.int32, (groups, slots), 1)
    member = jnp.zeros((groups, slots), jnp.float32)
    for one in range(slots_ref.shape[1]):
        member += jnp.where(slots_ref[:, one : one + 1] == spots, 1.0, 0.0)
    sums[my_dp] = lax.dot_general(
        member, key_rows[...], NN,
        precision=lax.Precision.HIGHEST, preferred_element_type=jnp.float32,
    )
    for step in range(1, dp_size):
        target = lax.rem(my_dp + step, dp_size)
        pltpu.make_async_remote_copy(
            src_ref=sums.at[my_dp],
            dst_ref=sums.at[my_dp],
            send_sem=sum_send.at[step],
            recv_sem=sum_recv.at[step],
            device_id=(target, me),
            device_id_type=MESH,
        ).start()

    for step in range(1, dp_size):
        source_dp = lax.rem(my_dp - step + dp_size, dp_size)
        swap = pltpu.make_async_remote_copy(
            src_ref=sums.at[my_dp],
            dst_ref=sums.at[source_dp],
            send_sem=sum_send.at[step],
            recv_sem=sum_recv.at[step],
            device_id=(lax.rem(my_dp + step, dp_size), me),
            device_id_type=MESH,
        )
        swap.wait_recv()
        swap.wait_send()
    total = sums[0]
    for one in range(1, dp_size):
        total = total + sums[one]
    next_ref[...] = decay_rate * cent_ref[...] + (1.0 - decay_rate) * total

    for at, result in enumerate(results):
        moved = bytes_of(at)
        pltpu.make_async_copy(moved, moved, in_send.at[at]).wait()
        pltpu.make_async_copy(moved, moved, back_recv.at[at]).wait()
        pltpu.make_async_copy(moved, moved, back_send.at[at]).wait()
        pltpu.make_async_copy(
            back.at[at, rows_of(me)], result.at[:, :, columns(me)], back_own.at[at]
        ).wait()


def settle_kernel(*refs):
    held, results, staged, loaded, stored = refs[:5], refs[5:10], refs[10:15], refs[15], refs[16]
    loads = [
        pltpu.make_async_copy(held[at], staged[at], loaded.at[at]) for at in range(5)
    ]
    stores = [
        pltpu.make_async_copy(staged[at], results[at], stored.at[at]) for at in range(5)
    ]
    for load in loads:
        load.start()
    for load, store in zip(loads, stores):
        load.wait()
        store.start()
    for store in stores:
        store.wait()


def per_device(queries, keys, values, cotangent, cluster_of, block_list, centroid_sums):
    seq_size = lax.axis_size("seq")
    dp_size = lax.axis_size("dp")
    head_count = cluster_of.shape[1]
    block_count = cluster_of.shape[2]
    token_count = queries.shape[1]
    block_len = token_count // block_count
    head_dim = centroid_sums.shape[1]
    groups_here = block_list.shape[1]
    cluster_cap = block_list.shape[2]
    owner_count = seq_size // head_count
    slot_cap = min(block_count, max(1, 2 * block_count // owner_count))
    slots = seq_size * slot_cap
    reach = -(-(cluster_cap - 1) // PAIR) * PAIR
    members = block_list[0]
    present = members >= 0
    if owner_count == 1:
        slot_table = members

        def pack(source):
            return source.reshape(block_count, block_len, seq_size * head_dim)

        def unpack(returned):
            return returned.reshape(1, token_count, head_count * head_dim)

    else:
        owner_local = cluster_of[0] // groups_here
        earlier = jnp.arange(block_count)[:, None] < jnp.arange(block_count)[None, :]
        same_owner = owner_local[:, :, None] == owner_local[:, None, :]
        slot_of = jnp.sum(same_owner & earlier[None], axis=1)
        selector = owner_local[:, None, None, :] == jnp.arange(owner_count)[None, :, None, None]
        selector = selector & (slot_of[:, None, None, :] == jnp.arange(slot_cap)[None, None, :, None])
        selector = selector.astype(jnp.bfloat16)

        def pack(source):
            blocks_in = source[0].reshape(block_count, block_len, head_count, head_dim)
            outgoing = jnp.einsum(
                "hlcj,jthd->cthld", selector, blocks_in, preferred_element_type=jnp.float32
            )
            return outgoing.astype(jnp.bfloat16).reshape(slot_cap, block_len, seq_size * head_dim)

        def unpack(returned):
            arranged = returned.reshape(slot_cap, block_len, head_count, owner_count, head_dim)
            gathered = jnp.einsum(
                "hlcj,cthld->jthd", selector, arranged, preferred_element_type=jnp.float32
            )
            return gathered.astype(jnp.bfloat16).reshape(1, token_count, head_count * head_dim)

        flat = members.reshape(-1)
        source_dev = jnp.where(flat >= 0, flat // block_count, -1)
        before = (
            (flat >= 0)[None, :]
            & (source_dev[None, :] == source_dev[:, None])
            & (flat[None, :] < flat[:, None])
        )
        slot_at = jnp.sum(before, axis=1)
        slot_table = jnp.where(flat >= 0, source_dev * slot_cap + slot_at, -1)
        slot_table = slot_table.reshape(members.shape).astype(jnp.int32)

    spots = jnp.arange(slots, dtype=jnp.int32)
    holds = slot_table.reshape(-1)[:, None] == spots[None, :]
    place = jnp.arange(holds.shape[0], dtype=jnp.int32)
    place_of = jnp.sum(jnp.where(holds, place[:, None] + 1, 0), axis=0)
    place_of = jnp.where(place_of > 0, place_of - 1, (groups_here + spots) * cluster_cap)
    rank = jnp.sum(place_of[None, :] < place_of[:, None], axis=1).astype(jnp.int32)
    cluster_at = place_of // cluster_cap
    first_slot = jnp.sum(cluster_at[None, :] < cluster_at[:, None], axis=1).astype(jnp.int32)
    at_rank = rank[None, :] == spots[:, None]
    order = jnp.sum(jnp.where(at_rank, spots[None, :], 0), axis=1).astype(jnp.int32)
    first = jnp.sum(jnp.where(at_rank, first_slot[None, :], 0), axis=1).astype(jnp.int32)

    lead = reach * block_len
    any_spec = pl.BlockSpec(memory_space=pl.ANY)
    smem_spec = pl.BlockSpec(memory_space=pltpu.SMEM)
    vmem_spec = pl.BlockSpec(memory_space=pltpu.VMEM)
    packed_shape = jax.ShapeDtypeStruct((slot_cap, block_len, seq_size * head_dim), jnp.bfloat16)
    results = pl.pallas_call(
        functools.partial(
            routed_kernel, seq_size, dp_size, slot_cap, block_len, head_dim, reach
        ),
        out_shape=(packed_shape,) * 4
        + (jax.ShapeDtypeStruct((groups_here, head_dim), jnp.float32),),
        in_specs=[smem_spec] * 3 + [vmem_spec] * 2 + [pl.BlockSpec(memory_space=pltpu.HBM)] * 4,
        out_specs=(any_spec,) * 4 + (vmem_spec,),
        scratch_shapes=[
            *[pltpu.VMEM((slots, block_len, head_dim), jnp.bfloat16)] * 4,
            pltpu.VMEM((4, lead + slots * block_len, head_dim), jnp.bfloat16),
            pltpu.VMEM((slots // PAIR, PAIR * block_len, lead + PAIR * block_len), jnp.float32),
            pltpu.VMEM((slots // PAIR, PAIR * block_len, head_dim), jnp.float32),
            pltpu.VMEM((lead + slots * block_len, head_dim), jnp.float32),
            pltpu.VMEM((lead + slots * block_len, head_dim), jnp.float32),
            pltpu.VMEM((4, slots, block_len, head_dim), jnp.bfloat16),
            pltpu.VMEM((4, slots, block_len, head_dim), jnp.bfloat16),
            pltpu.VMEM((slots, head_dim), jnp.float32),
            pltpu.VMEM((dp_size, groups_here, head_dim), jnp.float32),
        ]
        + [pltpu.SemaphoreType.DMA((4,))] * 6
        + [pltpu.SemaphoreType.DMA((dp_size,))] * 2,
        compiler_params=pltpu.CompilerParams(
            collective_id=0, has_side_effects=True, vmem_limit_bytes=60 * 1024 * 1024
        ),
    )(
        order, rank, first, slot_table, centroid_sums,
        pack(keys), pack(queries), pack(values), pack(cotangent),
    )
    if owner_count == 1:
        results = pl.pallas_call(
            settle_kernel,
            out_shape=tuple(jax.ShapeDtypeStruct(item.shape, item.dtype) for item in results),
            in_specs=[any_spec] * 5,
            out_specs=(any_spec,) * 5,
            scratch_shapes=[pltpu.VMEM(item.shape, item.dtype) for item in results]
            + [pltpu.SemaphoreType.DMA((5,))] * 2,
            compiler_params=pltpu.CompilerParams(vmem_limit_bytes=60 * 1024 * 1024),
        )(*results)
    return tuple(unpack(item) for item in results[:4]) + (results[4],)


def solution(mesh):
    in_specs = (
        P("dp", "seq", None),
        P("dp", "seq", None),
        P("dp", "seq", None),
        P("dp", "seq", None),
        P("dp", None, "seq"),
        P("dp", "seq", None),
        P("seq", None),
    )
    out_specs = (
        P("dp", "seq", None),
        P("dp", "seq", None),
        P("dp", "seq", None),
        P("dp", "seq", None),
        P("seq", None),
    )
    return jax.shard_map(
        per_device, mesh=mesh, in_specs=in_specs, out_specs=out_specs, check_vma=False
    )
```

```python
import functools
import math

import jax
import jax.numpy as jnp
from jax import lax
from jax.experimental import pallas as pl
from jax.experimental.pallas import tpu as pltpu
from jax.sharding import PartitionSpec as P

decay_rate = 0.99
neg_fill = -1e30
MESH = pl.DeviceIdType.MESH
PAIR = 2
NT = (((1,), (1,)), ((), ()))
TN = (((0,), (0,)), ((), ()))
NN = (((1,), (0,)), ((), ()))


def dot_f32(a, b, dims):
    return lax.dot_general(a, b, dims, preferred_element_type=jnp.float32)


def routed_kernel(
    seq_size, dp_size, slot_cap, block_len, head_dim, reach,
    slots_ref, cent_ref, k_ref, q_ref, v_ref, d_ref,
    out_ref, gq_ref, gk_ref, gv_ref, next_ref,
    k_in, q_in, v_in, d_in, ordered, probs_at, full_at, acc_k, acc_v, made, back, key_rows, sums, drawn, table,
    in_send, in_recv, in_own, back_send, back_recv, back_own, sum_send, sum_recv, table_sem,
):
    my_dp = lax.axis_index("dp")
    me = lax.axis_index("seq")
    slots = seq_size * slot_cap
    others = (seq_size - 1) * slot_cap
    lead = reach * block_len
    tile = PAIR * block_len
    window = lead + tile
    score_scale = 1.0 / math.sqrt(head_dim)

    barrier = pltpu.get_barrier_semaphore()

    def greet(step, carry):
        pl.semaphore_signal(
            barrier, inc=1, device_id=(my_dp, lax.rem(me + step, seq_size)), device_id_type=MESH
        )
        return carry

    lax.fori_loop(1, seq_size, greet, 0)
    for step in range(1, dp_size):
        pl.semaphore_signal(
            barrier, inc=1, device_id=(lax.rem(my_dp + step, dp_size), me), device_id_type=MESH
        )
    pl.semaphore_wait(barrier, seq_size + dp_size - 2)

    def partner(step):
        if seq_size & (seq_size - 1):
            return lax.rem(me + step, seq_size)
        odd = lax.rem(step, 2)
        offset = odd * (seq_size // 2) + step // 2
        target = 0
        for bit in range(seq_size.bit_length() - 1):
            mine = lax.rem(me // (1 << bit), 2)
            other = lax.rem(offset // (1 << bit), 2)
            target = target + (mine + other - 2 * mine * other) * (1 << bit)
        return target

    def columns(index):
        return pl.ds(pl.multiple_of(index * head_dim, head_dim), head_dim)

    def rows_of(index):
        return pl.ds(index * slot_cap, slot_cap)

    sources = (k_ref, q_ref, v_ref, d_ref)
    arrived = (k_in, q_in, v_in, d_in)
    def send_out(at):
        source = sources[at]
        pltpu.make_async_copy(
            source.at[:, :, columns(me)], arrived[at].at[rows_of(me)], in_own.at[at]
        ).start()

        def send(step, carry):
            target = partner(step)
            pltpu.make_async_remote_copy(
                src_ref=source.at[:, :, columns(target)],
                dst_ref=arrived[at].at[rows_of(me)],
                send_sem=in_send.at[at],
                recv_sem=in_recv.at[at],
                device_id=(my_dp, target),
                device_id_type=MESH,
            ).start()
            return carry

        lax.fori_loop(1, seq_size, send, 0)

    send_out(0)
    send_out(1)

    cap, groups = slots_ref.shape
    lanes = drawn.shape[1]
    slot_at = lax.broadcasted_iota(jnp.int32, (slots, groups), 0)
    group_at = lax.broadcasted_iota(jnp.int32, (slots, groups), 1)
    place_col = jnp.zeros((slots, 1), jnp.int32)
    group_col = jnp.zeros((slots, 1), jnp.int32)
    member = jnp.zeros((slots, groups), jnp.float32)
    for one in range(cap):
        holds = slots_ref[one : one + 1, :] == slot_at
        member += jnp.where(holds, 1.0, 0.0)
        place_col += jnp.sum(
            jnp.where(holds, group_at * cap + one + 1, 0), axis=1, keepdims=True
        )
        group_col += jnp.sum(jnp.where(holds, group_at + 1, 0), axis=1, keepdims=True)
    spot_col = lax.broadcasted_iota(jnp.int32, (slots, 1), 0)
    place_col = jnp.where(place_col > 0, place_col, (groups + spot_col) * cap + 1)
    group_col = jnp.where(group_col > 0, group_col, groups + spot_col + 1)
    spot_at = lax.broadcasted_iota(jnp.int32, (slots, lanes), 0)
    lane_at = lax.broadcasted_iota(jnp.int32, (slots, lanes), 1)

    def lay(column):
        return jnp.sum(jnp.where(spot_at == lane_at, column, 0), axis=0, keepdims=True)

    def count(column):
        less = (lay(column) < column) & (lane_at < slots)
        return jnp.sum(jnp.where(less, 1, 0), axis=1, keepdims=True)

    rank_col = count(place_col)
    first_col = count(group_col)
    at_rank = rank_col == lane_at
    drawn[...] = jnp.zeros_like(drawn)
    drawn[0:1, :] = jnp.sum(jnp.where(at_rank, spot_at, 0), axis=0, keepdims=True)
    drawn[1:2, :] = lay(rank_col)
    drawn[2:3, :] = jnp.sum(jnp.where(at_rank, first_col, 0), axis=0, keepdims=True)
    fill = pltpu.make_async_copy(drawn, table, table_sem.at[0])
    fill.start()
    fill.wait()

    ordered[:, :lead, :] = jnp.zeros((4, lead, head_dim), jnp.bfloat16)
    acc_k[...] = jnp.zeros_like(acc_k)
    acc_v[...] = jnp.zeros_like(acc_v)

    def bytes_of(at):
        return arrived[at].at[pl.ds(0, others)]

    def collect(at):
        part = bytes_of(at)
        pltpu.make_async_copy(part, part, in_recv.at[at]).wait()
        pltpu.make_async_copy(
            sources[at].at[:, :, columns(me)], arrived[at].at[rows_of(me)], in_own.at[at]
        ).wait()

        def place(spot, carry):
            rows = pl.ds(pl.multiple_of(lead + spot * block_len, block_len), block_len)
            ordered[at, rows, :] = arrived[at][table[0, spot]]
            return carry

        lax.fori_loop(0, slots, place, 0, unroll=4)

    results = (out_ref, gq_ref, gk_ref, gv_ref)

    def give_back(at):
        result = results[at]

        def settle(spot, carry):
            back[at, spot] = made[at, table[1, spot]]
            return carry

        lax.fori_loop(0, slots, settle, 0, unroll=4)
        pltpu.make_async_copy(
            back.at[at, rows_of(me)], result.at[:, :, columns(me)], back_own.at[at]
        ).start()

        def give(step, carry):
            target = partner(step)
            pltpu.make_async_remote_copy(
                src_ref=back.at[at, rows_of(target)],
                dst_ref=result.at[:, :, columns(me)],
                send_sem=back_send.at[at],
                recv_sem=back_recv.at[at],
                device_id=(my_dp, target),
                device_id_type=MESH,
            ).start()
            return carry

        lax.fori_loop(1, seq_size, give, 0)

    row_at = lax.broadcasted_iota(jnp.int32, (tile, window), 0)
    col_at = lax.broadcasted_iota(jnp.int32, (tile, window), 1)
    row_one = lax.broadcasted_iota(jnp.int32, (tile, 1), 0)
    tiled = (PAIR, block_len, head_dim)

    def spans(index):
        start = pl.multiple_of(index * tile, tile)
        own = pl.ds(pl.multiple_of(start + lead, block_len), tile)
        return own, pl.ds(start, window), pl.ds(index * PAIR, PAIR)

    def forward(index, carry):
        own, near, here = spans(index)
        low = jnp.zeros((tile, 1), jnp.int32)
        for one in range(PAIR):
            edge = lead + (table[2, index * PAIR + one] - index * PAIR) * block_len
            low = jnp.where(row_one >= one * block_len, edge, low)
        visible = (col_at <= row_at + lead) & (col_at >= low)
        scores = dot_f32(ordered[1, own, :], ordered[0, near, :], NT) * score_scale
        scores = jnp.where(visible, scores, neg_fill)
        raised = jnp.exp(scores - jnp.max(scores, axis=-1, keepdims=True))
        probs = raised / jnp.sum(raised, axis=-1, keepdims=True)
        out_full = dot_f32(probs.astype(jnp.bfloat16), ordered[2, near, :], NN)
        probs_at[index] = probs
        full_at[index] = out_full
        made[0, here] = out_full.astype(jnp.bfloat16).reshape(tiled)
        return carry

    def backward(index, carry):
        own, near, here = spans(index)
        k = ordered[0, near, :]
        q = ordered[1, own, :]
        g = ordered[3, own, :]
        probs = probs_at[index]
        dprobs = dot_f32(g, ordered[2, near, :], NT)
        row_dot = jnp.sum(g.astype(jnp.float32) * full_at[index], axis=-1, keepdims=True)
        dscores = (probs * (dprobs - row_dot) * score_scale).astype(jnp.bfloat16)
        made[1, here] = dot_f32(dscores, k, NN).astype(jnp.bfloat16).reshape(tiled)
        acc_k[near, :] += dot_f32(dscores, q, TN)
        return carry

    def backward_v(index, carry):
        own, near, here = spans(index)
        acc_v[near, :] += dot_f32(probs_at[index].astype(jnp.bfloat16), ordered[3, own, :], TN)
        return carry

    def wait_sent(at):
        moved = bytes_of(at)
        pltpu.make_async_copy(moved, moved, in_send.at[at]).wait()

    wait_sent(0)
    send_out(2)
    wait_sent(1)
    send_out(3)
    collect(0)
    collect(1)
    collect(2)
    lax.fori_loop(0, slots // PAIR, forward, 0, unroll=4)
    give_back(0)
    collect(3)
    lax.fori_loop(0, slots // PAIR, backward_v, 0, unroll=2)
    made[3] = acc_v[lead:, :].astype(jnp.bfloat16).reshape(slots, block_len, head_dim)
    give_back(3)
    lax.fori_loop(0, slots // PAIR, backward, 0, unroll=2)
    give_back(1)
    made[2] = acc_k[lead:, :].astype(jnp.bfloat16).reshape(slots, block_len, head_dim)
    give_back(2)

    def add_keys(spot, carry):
        key_rows[pl.ds(spot, 1), :] = jnp.sum(
            k_in[spot].astype(jnp.float32), axis=0, keepdims=True
        )
        return carry

    lax.fori_loop(0, slots, add_keys, 0)
    sums[my_dp] = lax.dot_general(
        member, key_rows[...], TN,
        precision=lax.Precision.HIGHEST, preferred_element_type=jnp.float32,
    )
    for step in range(1, dp_size):
        target = lax.rem(my_dp + step, dp_size)
        pltpu.make_async_remote_copy(
            src_ref=sums.at[my_dp],
            dst_ref=sums.at[my_dp],
            send_sem=sum_send.at[step],
            recv_sem=sum_recv.at[step],
            device_id=(target, me),
            device_id_type=MESH,
        ).start()

    for step in range(1, dp_size):
        source_dp = lax.rem(my_dp - step + dp_size, dp_size)
        swap = pltpu.make_async_remote_copy(
            src_ref=sums.at[my_dp],
            dst_ref=sums.at[source_dp],
            send_sem=sum_send.at[step],
            recv_sem=sum_recv.at[step],
            device_id=(lax.rem(my_dp + step, dp_size), me),
            device_id_type=MESH,
        )
        swap.wait_recv()
        swap.wait_send()
    total = sums[0]
    for one in range(1, dp_size):
        total = total + sums[one]
    next_ref[...] = decay_rate * cent_ref[...] + (1.0 - decay_rate) * total

    for at, result in enumerate(results):
        if at > 1:
            wait_sent(at)
        moved = bytes_of(at)
        pltpu.make_async_copy(moved, moved, back_recv.at[at]).wait()
        pltpu.make_async_copy(moved, moved, back_send.at[at]).wait()
        pltpu.make_async_copy(
            back.at[at, rows_of(me)], result.at[:, :, columns(me)], back_own.at[at]
        ).wait()


def settle_kernel(*refs):
    held, results, staged, loaded, stored = refs[:5], refs[5:10], refs[10:15], refs[15], refs[16]
    loads = [
        pltpu.make_async_copy(held[at], staged[at], loaded.at[at]) for at in range(5)
    ]
    stores = [
        pltpu.make_async_copy(staged[at], results[at], stored.at[at]) for at in range(5)
    ]
    for load in loads:
        load.start()
    for load, store in zip(loads, stores):
        load.wait()
        store.start()
    for store in stores:
        store.wait()


def per_device(queries, keys, values, cotangent, cluster_of, block_list, centroid_sums):
    seq_size = lax.axis_size("seq")
    dp_size = lax.axis_size("dp")
    head_count = cluster_of.shape[1]
    block_count = cluster_of.shape[2]
    token_count = queries.shape[1]
    block_len = token_count // block_count
    head_dim = centroid_sums.shape[1]
    groups_here = block_list.shape[1]
    cluster_cap = block_list.shape[2]
    owner_count = seq_size // head_count
    slot_cap = min(block_count, max(1, 2 * block_count // owner_count))
    slots = seq_size * slot_cap
    reach = -(-(cluster_cap - 1) // PAIR) * PAIR
    members = block_list[0]
    present = members >= 0
    if owner_count == 1:
        slot_table = members

        def pack(source):
            return source.reshape(block_count, block_len, seq_size * head_dim)

        def unpack(returned):
            return returned.reshape(1, token_count, head_count * head_dim)

    else:
        owner_local = cluster_of[0] // groups_here
        earlier = jnp.arange(block_count)[:, None] < jnp.arange(block_count)[None, :]
        same_owner = owner_local[:, :, None] == owner_local[:, None, :]
        slot_of = jnp.sum(same_owner & earlier[None], axis=1)
        selector = owner_local[:, None, None, :] == jnp.arange(owner_count)[None, :, None, None]
        selector = selector & (slot_of[:, None, None, :] == jnp.arange(slot_cap)[None, None, :, None])
        selector = selector.astype(jnp.bfloat16)

        def pack(source):
            blocks_in = source[0].reshape(block_count, block_len, head_count, head_dim)
            outgoing = jnp.einsum(
                "hlcj,jthd->cthld", selector, blocks_in, preferred_element_type=jnp.float32
            )
            return outgoing.astype(jnp.bfloat16).reshape(slot_cap, block_len, seq_size * head_dim)

        def unpack(returned):
            arranged = returned.reshape(slot_cap, block_len, head_count, owner_count, head_dim)
            gathered = jnp.einsum(
                "hlcj,cthld->jthd", selector, arranged, preferred_element_type=jnp.float32
            )
            return gathered.astype(jnp.bfloat16).reshape(1, token_count, head_count * head_dim)

        flat = members.reshape(-1)
        source_dev = jnp.where(flat >= 0, flat // block_count, -1)
        before = (
            (flat >= 0)[None, :]
            & (source_dev[None, :] == source_dev[:, None])
            & (flat[None, :] < flat[:, None])
        )
        slot_at = jnp.sum(before, axis=1)
        slot_table = jnp.where(flat >= 0, source_dev * slot_cap + slot_at, -1)
        slot_table = slot_table.reshape(members.shape).astype(jnp.int32)

    lead = reach * block_len
    lanes = -(-slots // 128) * 128
    any_spec = pl.BlockSpec(memory_space=pl.ANY)
    vmem_spec = pl.BlockSpec(memory_space=pltpu.VMEM)
    packed_shape = jax.ShapeDtypeStruct((slot_cap, block_len, seq_size * head_dim), jnp.bfloat16)
    results = pl.pallas_call(
        functools.partial(
            routed_kernel, seq_size, dp_size, slot_cap, block_len, head_dim, reach
        ),
        out_shape=(packed_shape,) * 4
        + (jax.ShapeDtypeStruct((groups_here, head_dim), jnp.float32),),
        in_specs=[vmem_spec] * 2 + [pl.BlockSpec(memory_space=pltpu.HBM)] * 4,
        out_specs=(any_spec,) * 4 + (vmem_spec,),
        scratch_shapes=[
            *[pltpu.VMEM((slots, block_len, head_dim), jnp.bfloat16)] * 4,
            pltpu.VMEM((4, lead + slots * block_len, head_dim), jnp.bfloat16),
            pltpu.VMEM((slots // PAIR, PAIR * block_len, lead + PAIR * block_len), jnp.float32),
            pltpu.VMEM((slots // PAIR, PAIR * block_len, head_dim), jnp.float32),
            pltpu.VMEM((lead + slots * block_len, head_dim), jnp.float32),
            pltpu.VMEM((lead + slots * block_len, head_dim), jnp.float32),
            pltpu.VMEM((4, slots, block_len, head_dim), jnp.bfloat16),
            pltpu.VMEM((4, slots, block_len, head_dim), jnp.bfloat16),
            pltpu.VMEM((slots, head_dim), jnp.float32),
            pltpu.VMEM((dp_size, groups_here, head_dim), jnp.float32),
            pltpu.VMEM((8, lanes), jnp.int32),
            pltpu.SMEM((8, lanes), jnp.int32),
        ]
        + [pltpu.SemaphoreType.DMA((4,))] * 6
        + [pltpu.SemaphoreType.DMA((dp_size,))] * 2
        + [pltpu.SemaphoreType.DMA((1,))],
        compiler_params=pltpu.CompilerParams(
            collective_id=0, has_side_effects=True, vmem_limit_bytes=60 * 1024 * 1024
        ),
    )(
        slot_table.T, centroid_sums,
        pack(keys), pack(queries), pack(values), pack(cotangent),
    )
    if owner_count == 1:
        results = pl.pallas_call(
            settle_kernel,
            out_shape=tuple(jax.ShapeDtypeStruct(item.shape, item.dtype) for item in results),
            in_specs=[any_spec] * 5,
            out_specs=(any_spec,) * 5,
            scratch_shapes=[pltpu.VMEM(item.shape, item.dtype) for item in results]
            + [pltpu.SemaphoreType.DMA((5,))] * 2,
            compiler_params=pltpu.CompilerParams(vmem_limit_bytes=60 * 1024 * 1024),
        )(*results)
    return tuple(unpack(item) for item in results[:4]) + (results[4],)


def solution(mesh):
    in_specs = (
        P("dp", "seq", None),
        P("dp", "seq", None),
        P("dp", "seq", None),
        P("dp", "seq", None),
        P("dp", None, "seq"),
        P("dp", "seq", None),
        P("seq", None),
    )
    out_specs = (
        P("dp", "seq", None),
        P("dp", "seq", None),
        P("dp", "seq", None),
        P("dp", "seq", None),
        P("seq", None),
    )
    return jax.shard_map(
        per_device, mesh=mesh, in_specs=in_specs, out_specs=out_specs, check_vma=False
    )
```

```python
import functools
import math

import jax
import jax.numpy as jnp
from jax import lax
from jax.experimental import pallas as pl
from jax.experimental.pallas import tpu as pltpu
from jax.sharding import PartitionSpec as P

decay_rate = 0.99
neg_fill = -1e30
MESH = pl.DeviceIdType.MESH
PAIR = 2
NT = (((1,), (1,)), ((), ()))
TN = (((0,), (0,)), ((), ()))
NN = (((1,), (0,)), ((), ()))


def dot_f32(a, b, dims):
    return lax.dot_general(a, b, dims, preferred_element_type=jnp.float32)


def routed_kernel(
    seq_size, dp_size, slot_cap, block_len, head_dim, reach,
    slots_ref, cent_ref, k_ref, q_ref, v_ref, d_ref,
    out_ref, gq_ref, gk_ref, gv_ref, next_ref,
    k_in, q_in, v_in, d_in, ordered, probs_at, full_at, acc_k, acc_v, made, back, key_rows, sums, drawn, table,
    in_send, in_recv, in_own, back_send, back_recv, back_own, sum_send, sum_recv, table_sem,
):
    my_dp = lax.axis_index("dp")
    me = lax.axis_index("seq")
    slots = seq_size * slot_cap
    others = (seq_size - 1) * slot_cap
    lead = reach * block_len
    tile = PAIR * block_len
    window = lead + tile
    score_scale = 1.0 / math.sqrt(head_dim)

    barrier = pltpu.get_barrier_semaphore()

    def greet(step, carry):
        pl.semaphore_signal(
            barrier, inc=1, device_id=(my_dp, lax.rem(me + step, seq_size)), device_id_type=MESH
        )
        return carry

    lax.fori_loop(1, seq_size, greet, 0)
    for step in range(1, dp_size):
        pl.semaphore_signal(
            barrier, inc=1, device_id=(lax.rem(my_dp + step, dp_size), me), device_id_type=MESH
        )
    pl.semaphore_wait(barrier, seq_size + dp_size - 2)

    def partner(step):
        if seq_size & (seq_size - 1):
            return lax.rem(me + step, seq_size)
        odd = lax.rem(step, 2)
        offset = odd * (seq_size // 2) + step // 2
        target = 0
        for bit in range(seq_size.bit_length() - 1):
            mine = lax.rem(me // (1 << bit), 2)
            other = lax.rem(offset // (1 << bit), 2)
            target = target + (mine + other - 2 * mine * other) * (1 << bit)
        return target

    def columns(index):
        return pl.ds(pl.multiple_of(index * head_dim, head_dim), head_dim)

    def rows_of(index):
        return pl.ds(index * slot_cap, slot_cap)

    sources = (k_ref, q_ref, v_ref, d_ref)
    arrived = (k_in, q_in, v_in, d_in)
    def send_out(at):
        source = sources[at]
        pltpu.make_async_copy(
            source.at[:, :, columns(me)], arrived[at].at[rows_of(me)], in_own.at[at]
        ).start()

        def send(step, carry):
            target = partner(step)
            pltpu.make_async_remote_copy(
                src_ref=source.at[:, :, columns(target)],
                dst_ref=arrived[at].at[rows_of(me)],
                send_sem=in_send.at[at],
                recv_sem=in_recv.at[at],
                device_id=(my_dp, target),
                device_id_type=MESH,
            ).start()
            return carry

        lax.fori_loop(1, seq_size, send, 0)

    send_out(0)
    send_out(1)
    send_out(2)

    cap, groups = slots_ref.shape
    lanes = drawn.shape[1]
    slot_at = lax.broadcasted_iota(jnp.int32, (slots, groups), 0)
    group_at = lax.broadcasted_iota(jnp.int32, (slots, groups), 1)
    place_col = jnp.zeros((slots, 1), jnp.int32)
    group_col = jnp.zeros((slots, 1), jnp.int32)
    member = jnp.zeros((slots, groups), jnp.float32)
    for one in range(cap):
        holds = slots_ref[one : one + 1, :] == slot_at
        member += jnp.where(holds, 1.0, 0.0)
        place_col += jnp.sum(
            jnp.where(holds, group_at * cap + one + 1, 0), axis=1, keepdims=True
        )
        group_col += jnp.sum(jnp.where(holds, group_at + 1, 0), axis=1, keepdims=True)
    spot_col = lax.broadcasted_iota(jnp.int32, (slots, 1), 0)
    place_col = jnp.where(place_col > 0, place_col, (groups + spot_col) * cap + 1)
    group_col = jnp.where(group_col > 0, group_col, groups + spot_col + 1)
    spot_at = lax.broadcasted_iota(jnp.int32, (slots, lanes), 0)
    lane_at = lax.broadcasted_iota(jnp.int32, (slots, lanes), 1)

    def lay(column):
        return jnp.sum(jnp.where(spot_at == lane_at, column, 0), axis=0, keepdims=True)

    def count(column):
        less = (lay(column) < column) & (lane_at < slots)
        return jnp.sum(jnp.where(less, 1, 0), axis=1, keepdims=True)

    rank_col = count(place_col)
    first_col = count(group_col)
    at_rank = rank_col == lane_at
    drawn[...] = jnp.zeros_like(drawn)
    drawn[0:1, :] = jnp.sum(jnp.where(at_rank, spot_at, 0), axis=0, keepdims=True)
    drawn[1:2, :] = lay(rank_col)
    drawn[2:3, :] = jnp.sum(jnp.where(at_rank, first_col, 0), axis=0, keepdims=True)
    fill = pltpu.make_async_copy(drawn, table, table_sem.at[0])
    fill.start()
    fill.wait()

    ordered[:, :lead, :] = jnp.zeros((4, lead, head_dim), jnp.bfloat16)
    acc_k[...] = jnp.zeros_like(acc_k)
    acc_v[...] = jnp.zeros_like(acc_v)

    def bytes_of(at):
        return arrived[at].at[pl.ds(0, others)]

    def collect(at):
        part = bytes_of(at)
        pltpu.make_async_copy(part, part, in_recv.at[at]).wait()
        pltpu.make_async_copy(
            sources[at].at[:, :, columns(me)], arrived[at].at[rows_of(me)], in_own.at[at]
        ).wait()

        def place(spot, carry):
            rows = pl.ds(pl.multiple_of(lead + spot * block_len, block_len), block_len)
            ordered[at, rows, :] = arrived[at][table[0, spot]]
            return carry

        lax.fori_loop(0, slots, place, 0, unroll=4)

    results = (out_ref, gq_ref, gk_ref, gv_ref)

    def give_back(at):
        result = results[at]

        def settle(spot, carry):
            back[at, spot] = made[at, table[1, spot]]
            return carry

        lax.fori_loop(0, slots, settle, 0, unroll=4)
        pltpu.make_async_copy(
            back.at[at, rows_of(me)], result.at[:, :, columns(me)], back_own.at[at]
        ).start()

        def give(step, carry):
            target = partner(step)
            pltpu.make_async_remote_copy(
                src_ref=back.at[at, rows_of(target)],
                dst_ref=result.at[:, :, columns(me)],
                send_sem=back_send.at[at],
                recv_sem=back_recv.at[at],
                device_id=(my_dp, target),
                device_id_type=MESH,
            ).start()
            return carry

        lax.fori_loop(1, seq_size, give, 0)

    row_at = lax.broadcasted_iota(jnp.int32, (tile, window), 0)
    col_at = lax.broadcasted_iota(jnp.int32, (tile, window), 1)
    row_one = lax.broadcasted_iota(jnp.int32, (tile, 1), 0)
    tiled = (PAIR, block_len, head_dim)

    def spans(index):
        start = pl.multiple_of(index * tile, tile)
        own = pl.ds(pl.multiple_of(start + lead, block_len), tile)
        return own, pl.ds(start, window), pl.ds(index * PAIR, PAIR)

    def forward(index, carry):
        own, near, here = spans(index)
        low = jnp.zeros((tile, 1), jnp.int32)
        for one in range(PAIR):
            edge = lead + (table[2, index * PAIR + one] - index * PAIR) * block_len
            low = jnp.where(row_one >= one * block_len, edge, low)
        visible = (col_at <= row_at + lead) & (col_at >= low)
        scores = dot_f32(ordered[1, own, :], ordered[0, near, :], NT) * score_scale
        scores = jnp.where(visible, scores, neg_fill)
        raised = jnp.exp(scores - jnp.max(scores, axis=-1, keepdims=True))
        probs = raised / jnp.sum(raised, axis=-1, keepdims=True)
        out_full = dot_f32(probs.astype(jnp.bfloat16), ordered[2, near, :], NN)
        probs_at[index] = probs
        full_at[index] = out_full
        made[0, here] = out_full.astype(jnp.bfloat16).reshape(tiled)
        return carry

    def backward(index, carry):
        own, near, here = spans(index)
        k = ordered[0, near, :]
        q = ordered[1, own, :]
        g = ordered[3, own, :]
        probs = probs_at[index]
        dprobs = dot_f32(g, ordered[2, near, :], NT)
        row_dot = jnp.sum(g.astype(jnp.float32) * full_at[index], axis=-1, keepdims=True)
        dscores = (probs * (dprobs - row_dot) * score_scale).astype(jnp.bfloat16)
        made[1, here] = dot_f32(dscores, k, NN).astype(jnp.bfloat16).reshape(tiled)
        acc_k[near, :] += dot_f32(dscores, q, TN)
        return carry

    def backward_v(index, carry):
        own, near, here = spans(index)
        acc_v[near, :] += dot_f32(probs_at[index].astype(jnp.bfloat16), ordered[3, own, :], TN)
        return carry

    def wait_sent(at):
        moved = bytes_of(at)
        pltpu.make_async_copy(moved, moved, in_send.at[at]).wait()

    wait_sent(0)
    send_out(3)
    collect(0)
    collect(1)

    def add_keys(spot, carry):
        key_rows[pl.ds(spot, 1), :] = jnp.sum(
            k_in[spot].astype(jnp.float32), axis=0, keepdims=True
        )
        return carry

    lax.fori_loop(0, slots, add_keys, 0)
    sums[my_dp] = lax.dot_general(
        member, key_rows[...], TN,
        precision=lax.Precision.HIGHEST, preferred_element_type=jnp.float32,
    )
    for step in range(1, dp_size):
        target = lax.rem(my_dp + step, dp_size)
        pltpu.make_async_remote_copy(
            src_ref=sums.at[my_dp],
            dst_ref=sums.at[my_dp],
            send_sem=sum_send.at[step],
            recv_sem=sum_recv.at[step],
            device_id=(target, me),
            device_id_type=MESH,
        ).start()

    collect(2)
    lax.fori_loop(0, slots // PAIR, forward, 0, unroll=4)
    give_back(0)
    collect(3)
    lax.fori_loop(0, slots // PAIR, backward_v, 0, unroll=2)
    made[3] = acc_v[lead:, :].astype(jnp.bfloat16).reshape(slots, block_len, head_dim)
    give_back(3)
    lax.fori_loop(0, slots // PAIR, backward, 0, unroll=2)
    give_back(1)
    made[2] = acc_k[lead:, :].astype(jnp.bfloat16).reshape(slots, block_len, head_dim)
    give_back(2)

    for step in range(1, dp_size):
        source_dp = lax.rem(my_dp - step + dp_size, dp_size)
        swap = pltpu.make_async_remote_copy(
            src_ref=sums.at[my_dp],
            dst_ref=sums.at[source_dp],
            send_sem=sum_send.at[step],
            recv_sem=sum_recv.at[step],
            device_id=(lax.rem(my_dp + step, dp_size), me),
            device_id_type=MESH,
        )
        swap.wait_recv()
        swap.wait_send()
    total = sums[0]
    for one in range(1, dp_size):
        total = total + sums[one]
    next_ref[...] = decay_rate * cent_ref[...] + (1.0 - decay_rate) * total

    for at, result in enumerate(results):
        if at > 0:
            wait_sent(at)
        moved = bytes_of(at)
        pltpu.make_async_copy(moved, moved, back_recv.at[at]).wait()
        pltpu.make_async_copy(moved, moved, back_send.at[at]).wait()
        pltpu.make_async_copy(
            back.at[at, rows_of(me)], result.at[:, :, columns(me)], back_own.at[at]
        ).wait()


def settle_kernel(*refs):
    held, results, staged, loaded, stored = refs[:5], refs[5:10], refs[10:15], refs[15], refs[16]
    loads, stores = [], []
    for at in range(5):
        rows = held[at].shape[0]
        half = max(1, rows // 2)
        for cut in range(rows // half):
            piece = pl.ds(cut * half, half)
            loads.append(pltpu.make_async_copy(
                held[at].at[piece], staged[at].at[piece], loaded.at[at, cut]
            ))
            stores.append(pltpu.make_async_copy(
                staged[at].at[piece], results[at].at[piece], stored.at[at, cut]
            ))
    for load in loads:
        load.start()
    for load, store in zip(loads, stores):
        load.wait()
        store.start()
    for store in stores:
        store.wait()


def per_device(queries, keys, values, cotangent, cluster_of, block_list, centroid_sums):
    seq_size = lax.axis_size("seq")
    dp_size = lax.axis_size("dp")
    head_count = cluster_of.shape[1]
    block_count = cluster_of.shape[2]
    token_count = queries.shape[1]
    block_len = token_count // block_count
    head_dim = centroid_sums.shape[1]
    groups_here = block_list.shape[1]
    cluster_cap = block_list.shape[2]
    owner_count = seq_size // head_count
    slot_cap = min(block_count, max(1, 2 * block_count // owner_count))
    slots = seq_size * slot_cap
    reach = -(-(cluster_cap - 1) // PAIR) * PAIR
    members = block_list[0]
    present = members >= 0
    if owner_count == 1:
        slot_table = members

        def pack(source):
            return source.reshape(block_count, block_len, seq_size * head_dim)

        def unpack(returned):
            return returned.reshape(1, token_count, head_count * head_dim)

    else:
        owner_local = cluster_of[0] // groups_here
        earlier = jnp.arange(block_count)[:, None] < jnp.arange(block_count)[None, :]
        same_owner = owner_local[:, :, None] == owner_local[:, None, :]
        slot_of = jnp.sum(same_owner & earlier[None], axis=1)
        selector = owner_local[:, None, None, :] == jnp.arange(owner_count)[None, :, None, None]
        selector = selector & (slot_of[:, None, None, :] == jnp.arange(slot_cap)[None, None, :, None])
        selector = selector.astype(jnp.bfloat16)

        def pack(source):
            blocks_in = source[0].reshape(block_count, block_len, head_count, head_dim)
            outgoing = jnp.einsum(
                "hlcj,jthd->cthld", selector, blocks_in, preferred_element_type=jnp.float32
            )
            return outgoing.astype(jnp.bfloat16).reshape(slot_cap, block_len, seq_size * head_dim)

        def unpack(returned):
            arranged = returned.reshape(slot_cap, block_len, head_count, owner_count, head_dim)
            gathered = jnp.einsum(
                "hlcj,cthld->jthd", selector, arranged, preferred_element_type=jnp.float32
            )
            return gathered.astype(jnp.bfloat16).reshape(1, token_count, head_count * head_dim)

        flat = members.reshape(-1)
        source_dev = jnp.where(flat >= 0, flat // block_count, -1)
        before = (
            (flat >= 0)[None, :]
            & (source_dev[None, :] == source_dev[:, None])
            & (flat[None, :] < flat[:, None])
        )
        slot_at = jnp.sum(before, axis=1)
        slot_table = jnp.where(flat >= 0, source_dev * slot_cap + slot_at, -1)
        slot_table = slot_table.reshape(members.shape).astype(jnp.int32)

    lead = reach * block_len
    lanes = -(-slots // 128) * 128
    any_spec = pl.BlockSpec(memory_space=pl.ANY)
    vmem_spec = pl.BlockSpec(memory_space=pltpu.VMEM)
    packed_shape = jax.ShapeDtypeStruct((slot_cap, block_len, seq_size * head_dim), jnp.bfloat16)
    results = pl.pallas_call(
        functools.partial(
            routed_kernel, seq_size, dp_size, slot_cap, block_len, head_dim, reach
        ),
        out_shape=(packed_shape,) * 4
        + (jax.ShapeDtypeStruct((groups_here, head_dim), jnp.float32),),
        in_specs=[vmem_spec] * 2 + [pl.BlockSpec(memory_space=pltpu.HBM)] * 4,
        out_specs=(any_spec,) * 4 + (vmem_spec,),
        scratch_shapes=[
            *[pltpu.VMEM((slots, block_len, head_dim), jnp.bfloat16)] * 4,
            pltpu.VMEM((4, lead + slots * block_len, head_dim), jnp.bfloat16),
            pltpu.VMEM((slots // PAIR, PAIR * block_len, lead + PAIR * block_len), jnp.float32),
            pltpu.VMEM((slots // PAIR, PAIR * block_len, head_dim), jnp.float32),
            pltpu.VMEM((lead + slots * block_len, head_dim), jnp.float32),
            pltpu.VMEM((lead + slots * block_len, head_dim), jnp.float32),
            pltpu.VMEM((4, slots, block_len, head_dim), jnp.bfloat16),
            pltpu.VMEM((4, slots, block_len, head_dim), jnp.bfloat16),
            pltpu.VMEM((slots, head_dim), jnp.float32),
            pltpu.VMEM((dp_size, groups_here, head_dim), jnp.float32),
            pltpu.VMEM((8, lanes), jnp.int32),
            pltpu.SMEM((8, lanes), jnp.int32),
        ]
        + [pltpu.SemaphoreType.DMA((4,))] * 6
        + [pltpu.SemaphoreType.DMA((dp_size,))] * 2
        + [pltpu.SemaphoreType.DMA((1,))],
        compiler_params=pltpu.CompilerParams(
            collective_id=0, has_side_effects=True, vmem_limit_bytes=60 * 1024 * 1024
        ),
    )(
        slot_table.T, centroid_sums,
        pack(keys), pack(queries), pack(values), pack(cotangent),
    )
    if owner_count == 1:
        results = pl.pallas_call(
            settle_kernel,
            out_shape=tuple(jax.ShapeDtypeStruct(item.shape, item.dtype) for item in results),
            in_specs=[any_spec] * 5,
            out_specs=(any_spec,) * 5,
            scratch_shapes=[pltpu.VMEM(item.shape, item.dtype) for item in results]
            + [pltpu.SemaphoreType.DMA((5, 2))] * 2,
            compiler_params=pltpu.CompilerParams(vmem_limit_bytes=60 * 1024 * 1024),
        )(*results)
    return tuple(unpack(item) for item in results[:4]) + (results[4],)


def solution(mesh):
    in_specs = (
        P("dp", "seq", None),
        P("dp", "seq", None),
        P("dp", "seq", None),
        P("dp", "seq", None),
        P("dp", None, "seq"),
        P("dp", "seq", None),
        P("seq", None),
    )
    out_specs = (
        P("dp", "seq", None),
        P("dp", "seq", None),
        P("dp", "seq", None),
        P("dp", "seq", None),
        P("seq", None),
    )
    return jax.shard_map(
        per_device, mesh=mesh, in_specs=in_specs, out_specs=out_specs, check_vma=False
    )
```

```python
import functools
import math

import jax
import jax.numpy as jnp
from jax import lax
from jax.experimental import pallas as pl
from jax.experimental.pallas import tpu as pltpu
from jax.sharding import PartitionSpec as P

decay_rate = 0.99
neg_fill = -1e30
MESH = pl.DeviceIdType.MESH
PAIR = 2
NT = (((1,), (1,)), ((), ()))
TN = (((0,), (0,)), ((), ()))
NN = (((1,), (0,)), ((), ()))


def dot_f32(a, b, dims):
    return lax.dot_general(a, b, dims, preferred_element_type=jnp.float32)


def routed_kernel(
    seq_size, dp_size, slot_cap, block_len, head_dim, reach,
    slots_ref, cent_ref, k_ref, q_ref, v_ref, d_ref,
    out_ref, gq_ref, gk_ref, gv_ref, next_ref,
    k_in, q_in, v_in, d_in, ordered, probs_at, full_at, acc_k, acc_v, made, back, key_rows, sums, drawn, table,
    in_send, in_recv, in_own, back_send, back_recv, back_own, sum_send, sum_recv, table_sem,
):
    my_dp = lax.axis_index("dp")
    me = lax.axis_index("seq")
    slots = seq_size * slot_cap
    others = (seq_size - 1) * slot_cap
    lead = reach * block_len
    tile = PAIR * block_len
    window = lead + tile
    score_scale = 1.0 / math.sqrt(head_dim)

    barrier = pltpu.get_barrier_semaphore()

    def greet(step, carry):
        pl.semaphore_signal(
            barrier, inc=1, device_id=(my_dp, lax.rem(me + step, seq_size)), device_id_type=MESH
        )
        return carry

    lax.fori_loop(1, seq_size, greet, 0)
    for step in range(1, dp_size):
        pl.semaphore_signal(
            barrier, inc=1, device_id=(lax.rem(my_dp + step, dp_size), me), device_id_type=MESH
        )
    pl.semaphore_wait(barrier, seq_size + dp_size - 2)

    def partner(step):
        if seq_size & (seq_size - 1):
            return lax.rem(me + step, seq_size)
        offset = seq_size - step
        target = 0
        for bit in range(seq_size.bit_length() - 1):
            mine = lax.rem(me // (1 << bit), 2)
            other = lax.rem(offset // (1 << bit), 2)
            target = target + (mine + other - 2 * mine * other) * (1 << bit)
        return target

    def columns(index):
        return pl.ds(pl.multiple_of(index * head_dim, head_dim), head_dim)

    def rows_of(index):
        return pl.ds(index * slot_cap, slot_cap)

    sources = (k_ref, q_ref, v_ref, d_ref)
    arrived = (k_in, q_in, v_in, d_in)
    def send_out(at):
        source = sources[at]
        pltpu.make_async_copy(
            source.at[:, :, columns(me)], arrived[at].at[rows_of(me)], in_own.at[at]
        ).start()

        def send(step, carry):
            target = partner(step)
            pltpu.make_async_remote_copy(
                src_ref=source.at[:, :, columns(target)],
                dst_ref=arrived[at].at[rows_of(me)],
                send_sem=in_send.at[at],
                recv_sem=in_recv.at[at],
                device_id=(my_dp, target),
                device_id_type=MESH,
            ).start()
            return carry

        lax.fori_loop(1, seq_size, send, 0)

    send_out(0)
    send_out(1)
    send_out(2)

    cap, groups = slots_ref.shape
    lanes = drawn.shape[1]
    slot_at = lax.broadcasted_iota(jnp.int32, (slots, groups), 0)
    group_at = lax.broadcasted_iota(jnp.int32, (slots, groups), 1)
    place_col = jnp.zeros((slots, 1), jnp.int32)
    group_col = jnp.zeros((slots, 1), jnp.int32)
    member = jnp.zeros((slots, groups), jnp.float32)
    for one in range(cap):
        holds = slots_ref[one : one + 1, :] == slot_at
        member += jnp.where(holds, 1.0, 0.0)
        place_col += jnp.sum(
            jnp.where(holds, group_at * cap + one + 1, 0), axis=1, keepdims=True
        )
        group_col += jnp.sum(jnp.where(holds, group_at + 1, 0), axis=1, keepdims=True)
    spot_col = lax.broadcasted_iota(jnp.int32, (slots, 1), 0)
    place_col = jnp.where(place_col > 0, place_col, (groups + spot_col) * cap + 1)
    group_col = jnp.where(group_col > 0, group_col, groups + spot_col + 1)
    spot_at = lax.broadcasted_iota(jnp.int32, (slots, lanes), 0)
    lane_at = lax.broadcasted_iota(jnp.int32, (slots, lanes), 1)

    def lay(column):
        return jnp.sum(jnp.where(spot_at == lane_at, column, 0), axis=0, keepdims=True)

    def count(column):
        less = (lay(column) < column) & (lane_at < slots)
        return jnp.sum(jnp.where(less, 1, 0), axis=1, keepdims=True)

    rank_col = count(place_col)
    first_col = count(group_col)
    at_rank = rank_col == lane_at
    drawn[...] = jnp.zeros_like(drawn)
    drawn[0:1, :] = jnp.sum(jnp.where(at_rank, spot_at, 0), axis=0, keepdims=True)
    drawn[1:2, :] = lay(rank_col)
    drawn[2:3, :] = jnp.sum(jnp.where(at_rank, first_col, 0), axis=0, keepdims=True)
    fill = pltpu.make_async_copy(drawn, table, table_sem.at[0])
    fill.start()
    fill.wait()

    ordered[:, :lead, :] = jnp.zeros((4, lead, head_dim), jnp.bfloat16)
    acc_k[...] = jnp.zeros_like(acc_k)
    acc_v[...] = jnp.zeros_like(acc_v)

    def bytes_of(at):
        return arrived[at].at[pl.ds(0, others)]

    def collect(at):
        part = bytes_of(at)
        pltpu.make_async_copy(part, part, in_recv.at[at]).wait()
        pltpu.make_async_copy(
            sources[at].at[:, :, columns(me)], arrived[at].at[rows_of(me)], in_own.at[at]
        ).wait()

        def place(spot, carry):
            rows = pl.ds(pl.multiple_of(lead + spot * block_len, block_len), block_len)
            ordered[at, rows, :] = arrived[at][table[0, spot]]
            return carry

        lax.fori_loop(0, slots, place, 0, unroll=4)

    results = (out_ref, gq_ref, gk_ref, gv_ref)

    def give_back(at):
        result = results[at]

        def settle(spot, carry):
            back[at, spot] = made[at, table[1, spot]]
            return carry

        lax.fori_loop(0, slots, settle, 0, unroll=4)
        pltpu.make_async_copy(
            back.at[at, rows_of(me)], result.at[:, :, columns(me)], back_own.at[at]
        ).start()

        def give(step, carry):
            target = partner(step)
            pltpu.make_async_remote_copy(
                src_ref=back.at[at, rows_of(target)],
                dst_ref=result.at[:, :, columns(me)],
                send_sem=back_send.at[at],
                recv_sem=back_recv.at[at],
                device_id=(my_dp, target),
                device_id_type=MESH,
            ).start()
            return carry

        lax.fori_loop(1, seq_size, give, 0)

    row_at = lax.broadcasted_iota(jnp.int32, (tile, window), 0)
    col_at = lax.broadcasted_iota(jnp.int32, (tile, window), 1)
    row_one = lax.broadcasted_iota(jnp.int32, (tile, 1), 0)
    tiled = (PAIR, block_len, head_dim)

    def spans(index):
        start = pl.multiple_of(index * tile, tile)
        own = pl.ds(pl.multiple_of(start + lead, block_len), tile)
        return own, pl.ds(start, window), pl.ds(index * PAIR, PAIR)

    def forward(index, carry):
        own, near, here = spans(index)
        low = jnp.zeros((tile, 1), jnp.int32)
        for one in range(PAIR):
            edge = lead + (table[2, index * PAIR + one] - index * PAIR) * block_len
            low = jnp.where(row_one >= one * block_len, edge, low)
        visible = (col_at <= row_at + lead) & (col_at >= low)
        scores = dot_f32(ordered[1, own, :], ordered[0, near, :], NT) * score_scale
        scores = jnp.where(visible, scores, neg_fill)
        raised = jnp.exp(scores - jnp.max(scores, axis=-1, keepdims=True))
        probs = raised / jnp.sum(raised, axis=-1, keepdims=True)
        out_full = dot_f32(probs.astype(jnp.bfloat16), ordered[2, near, :], NN)
        probs_at[index] = probs
        full_at[index] = out_full
        made[0, here] = out_full.astype(jnp.bfloat16).reshape(tiled)
        return carry

    def backward(index, carry):
        own, near, here = spans(index)
        k = ordered[0, near, :]
        q = ordered[1, own, :]
        g = ordered[3, own, :]
        probs = probs_at[index]
        dprobs = dot_f32(g, ordered[2, near, :], NT)
        row_dot = jnp.sum(g.astype(jnp.float32) * full_at[index], axis=-1, keepdims=True)
        dscores = (probs * (dprobs - row_dot) * score_scale).astype(jnp.bfloat16)
        made[1, here] = dot_f32(dscores, k, NN).astype(jnp.bfloat16).reshape(tiled)
        acc_k[near, :] += dot_f32(dscores, q, TN)
        return carry

    def backward_v(index, carry):
        own, near, here = spans(index)
        acc_v[near, :] += dot_f32(probs_at[index].astype(jnp.bfloat16), ordered[3, own, :], TN)
        return carry

    def wait_sent(at):
        moved = bytes_of(at)
        pltpu.make_async_copy(moved, moved, in_send.at[at]).wait()

    wait_sent(0)
    send_out(3)
    collect(0)
    collect(1)

    def add_keys(spot, carry):
        key_rows[pl.ds(spot, 1), :] = jnp.sum(
            k_in[spot].astype(jnp.float32), axis=0, keepdims=True
        )
        return carry

    lax.fori_loop(0, slots, add_keys, 0)
    sums[my_dp] = lax.dot_general(
        member, key_rows[...], TN,
        precision=lax.Precision.HIGHEST, preferred_element_type=jnp.float32,
    )
    for step in range(1, dp_size):
        target = lax.rem(my_dp + step, dp_size)
        pltpu.make_async_remote_copy(
            src_ref=sums.at[my_dp],
            dst_ref=sums.at[my_dp],
            send_sem=sum_send.at[step],
            recv_sem=sum_recv.at[step],
            device_id=(target, me),
            device_id_type=MESH,
        ).start()

    collect(2)
    lax.fori_loop(0, slots // PAIR, forward, 0, unroll=4)
    give_back(0)
    collect(3)
    lax.fori_loop(0, slots // PAIR, backward_v, 0, unroll=2)
    made[3] = acc_v[lead:, :].astype(jnp.bfloat16).reshape(slots, block_len, head_dim)
    give_back(3)
    lax.fori_loop(0, slots // PAIR, backward, 0, unroll=2)
    give_back(1)
    made[2] = acc_k[lead:, :].astype(jnp.bfloat16).reshape(slots, block_len, head_dim)
    give_back(2)

    for step in range(1, dp_size):
        source_dp = lax.rem(my_dp - step + dp_size, dp_size)
        swap = pltpu.make_async_remote_copy(
            src_ref=sums.at[my_dp],
            dst_ref=sums.at[source_dp],
            send_sem=sum_send.at[step],
            recv_sem=sum_recv.at[step],
            device_id=(lax.rem(my_dp + step, dp_size), me),
            device_id_type=MESH,
        )
        swap.wait_recv()
        swap.wait_send()
    total = sums[0]
    for one in range(1, dp_size):
        total = total + sums[one]
    next_ref[...] = decay_rate * cent_ref[...] + (1.0 - decay_rate) * total

    for at, result in enumerate(results):
        if at > 0:
            wait_sent(at)
        moved = bytes_of(at)
        pltpu.make_async_copy(moved, moved, back_recv.at[at]).wait()
        pltpu.make_async_copy(moved, moved, back_send.at[at]).wait()
        pltpu.make_async_copy(
            back.at[at, rows_of(me)], result.at[:, :, columns(me)], back_own.at[at]
        ).wait()


def settle_kernel(*refs):
    held, results, staged, loaded, stored = refs[:5], refs[5:10], refs[10:15], refs[15], refs[16]
    loads, stores = [], []
    for at in range(5):
        rows = held[at].shape[0]
        half = max(1, rows // 2)
        for cut in range(rows // half):
            piece = pl.ds(cut * half, half)
            loads.append(pltpu.make_async_copy(
                held[at].at[piece], staged[at].at[piece], loaded.at[at, cut]
            ))
            stores.append(pltpu.make_async_copy(
                staged[at].at[piece], results[at].at[piece], stored.at[at, cut]
            ))
    for load in loads:
        load.start()
    for load, store in zip(loads, stores):
        load.wait()
        store.start()
    for store in stores:
        store.wait()


def per_device(queries, keys, values, cotangent, cluster_of, block_list, centroid_sums):
    seq_size = lax.axis_size("seq")
    dp_size = lax.axis_size("dp")
    head_count = cluster_of.shape[1]
    block_count = cluster_of.shape[2]
    token_count = queries.shape[1]
    block_len = token_count // block_count
    head_dim = centroid_sums.shape[1]
    groups_here = block_list.shape[1]
    cluster_cap = block_list.shape[2]
    owner_count = seq_size // head_count
    slot_cap = min(block_count, max(1, 2 * block_count // owner_count))
    slots = seq_size * slot_cap
    reach = -(-(cluster_cap - 1) // PAIR) * PAIR
    members = block_list[0]
    present = members >= 0
    if owner_count == 1:
        slot_table = members

        def pack(source):
            return source.reshape(block_count, block_len, seq_size * head_dim)

        def unpack(returned):
            return returned.reshape(1, token_count, head_count * head_dim)

    else:
        owner_local = cluster_of[0] // groups_here
        earlier = jnp.arange(block_count)[:, None] < jnp.arange(block_count)[None, :]
        same_owner = owner_local[:, :, None] == owner_local[:, None, :]
        slot_of = jnp.sum(same_owner & earlier[None], axis=1)
        selector = owner_local[:, None, None, :] == jnp.arange(owner_count)[None, :, None, None]
        selector = selector & (slot_of[:, None, None, :] == jnp.arange(slot_cap)[None, None, :, None])
        selector = selector.astype(jnp.bfloat16)

        def pack(source):
            blocks_in = source[0].reshape(block_count, block_len, head_count, head_dim)
            outgoing = jnp.einsum(
                "hlcj,jthd->cthld", selector, blocks_in, preferred_element_type=jnp.float32
            )
            return outgoing.astype(jnp.bfloat16).reshape(slot_cap, block_len, seq_size * head_dim)

        def unpack(returned):
            arranged = returned.reshape(slot_cap, block_len, head_count, owner_count, head_dim)
            gathered = jnp.einsum(
                "hlcj,cthld->jthd", selector, arranged, preferred_element_type=jnp.float32
            )
            return gathered.astype(jnp.bfloat16).reshape(1, token_count, head_count * head_dim)

        flat = members.reshape(-1)
        source_dev = jnp.where(flat >= 0, flat // block_count, -1)
        before = (
            (flat >= 0)[None, :]
            & (source_dev[None, :] == source_dev[:, None])
            & (flat[None, :] < flat[:, None])
        )
        slot_at = jnp.sum(before, axis=1)
        slot_table = jnp.where(flat >= 0, source_dev * slot_cap + slot_at, -1)
        slot_table = slot_table.reshape(members.shape).astype(jnp.int32)

    lead = reach * block_len
    lanes = -(-slots // 128) * 128
    any_spec = pl.BlockSpec(memory_space=pl.ANY)
    vmem_spec = pl.BlockSpec(memory_space=pltpu.VMEM)
    packed_shape = jax.ShapeDtypeStruct((slot_cap, block_len, seq_size * head_dim), jnp.bfloat16)
    results = pl.pallas_call(
        functools.partial(
            routed_kernel, seq_size, dp_size, slot_cap, block_len, head_dim, reach
        ),
        out_shape=(packed_shape,) * 4
        + (jax.ShapeDtypeStruct((groups_here, head_dim), jnp.float32),),
        in_specs=[vmem_spec] * 2 + [pl.BlockSpec(memory_space=pltpu.HBM)] * 4,
        out_specs=(any_spec,) * 4 + (vmem_spec,),
        scratch_shapes=[
            *[pltpu.VMEM((slots, block_len, head_dim), jnp.bfloat16)] * 4,
            pltpu.VMEM((4, lead + slots * block_len, head_dim), jnp.bfloat16),
            pltpu.VMEM((slots // PAIR, PAIR * block_len, lead + PAIR * block_len), jnp.float32),
            pltpu.VMEM((slots // PAIR, PAIR * block_len, head_dim), jnp.float32),
            pltpu.VMEM((lead + slots * block_len, head_dim), jnp.float32),
            pltpu.VMEM((lead + slots * block_len, head_dim), jnp.float32),
            pltpu.VMEM((4, slots, block_len, head_dim), jnp.bfloat16),
            pltpu.VMEM((4, slots, block_len, head_dim), jnp.bfloat16),
            pltpu.VMEM((slots, head_dim), jnp.float32),
            pltpu.VMEM((dp_size, groups_here, head_dim), jnp.float32),
            pltpu.VMEM((8, lanes), jnp.int32),
            pltpu.SMEM((8, lanes), jnp.int32),
        ]
        + [pltpu.SemaphoreType.DMA((4,))] * 6
        + [pltpu.SemaphoreType.DMA((dp_size,))] * 2
        + [pltpu.SemaphoreType.DMA((1,))],
        compiler_params=pltpu.CompilerParams(
            collective_id=0, has_side_effects=True, vmem_limit_bytes=60 * 1024 * 1024
        ),
    )(
        slot_table.T, centroid_sums,
        pack(keys), pack(queries), pack(values), pack(cotangent),
    )
    if owner_count == 1:
        results = pl.pallas_call(
            settle_kernel,
            out_shape=tuple(jax.ShapeDtypeStruct(item.shape, item.dtype) for item in results),
            in_specs=[any_spec] * 5,
            out_specs=(any_spec,) * 5,
            scratch_shapes=[pltpu.VMEM(item.shape, item.dtype) for item in results]
            + [pltpu.SemaphoreType.DMA((5, 2))] * 2,
            compiler_params=pltpu.CompilerParams(vmem_limit_bytes=60 * 1024 * 1024),
        )(*results)
    return tuple(unpack(item) for item in results[:4]) + (results[4],)


def solution(mesh):
    in_specs = (
        P("dp", "seq", None),
        P("dp", "seq", None),
        P("dp", "seq", None),
        P("dp", "seq", None),
        P("dp", None, "seq"),
        P("dp", "seq", None),
        P("seq", None),
    )
    out_specs = (
        P("dp", "seq", None),
        P("dp", "seq", None),
        P("dp", "seq", None),
        P("dp", "seq", None),
        P("seq", None),
    )
    return jax.shard_map(
        per_device, mesh=mesh, in_specs=in_specs, out_specs=out_specs, check_vma=False
    )
```
